512 devices in a mesh: seg: 16 (over z_hi, x), coil: 32 (over y, z_lo, core).
Axes of the slice: x: 4, y: 4, z: 16 (z_hi: 4, z_lo: 4; z = z_hi * 4 + z_lo), core: 2. Of those that a mesh axis runs over, the one named last changes fastest.
Arguments:
- image_estimate: bfloat16 [1, 384, 768], replicated, may hold values from -6 to 6
- coil_maps: bfloat16 [32, 384, 768], P('coil'), may hold values from -3 to 3
- field_map: float32 [384, 384], replicated, may hold values from -3 to 3
- interp_rows: bfloat16 [1, 256, 384], replicated, may hold values from -0.3125 to 0.3125
- interp_cols: bfloat16 [1, 128, 384], replicated, may hold values from -0.3125 to 0.3125
- measured: bfloat16 [32, 1, 256, 256], P('coil'), may hold values from -6 to 6
- sample_time: int32 [1, 256], replicated, may hold values from 0 to 60
- sample_count: int32 [1], replicated, may hold values from 128 to 256
Outputs:
- gradient: float32 [1, 384, 768], P(None, 'coil', 'seg')
- residual: float32 [32, 1, 256, 256], P('coil', None, 'seg')
The draws below stay inside these ranges and needn't reach their ends.
Inputs may be any that keep to these rules, and one draw needn't show every extreme that they name: sample_time counts the sample clock, 4 steps to a segment. Rows below sample_count[p] of partition p are acquired.
All inputs are finite; a program needn't handle non-finite values.
Results may differ from the reference program's by a relative error of at most 0.017.
Values sent between devices are 32-bit elements; how exact they have to be, the bound alone decides.
A program may use at most 64 MiB of HBM per device.

```python
import jax
import jax.numpy as jnp
from jax import lax

NPIX = 384
SROWS = 256
SCOLS = 128
PARTS_SIZE = 1
SUBSTEPS = 4
NSEG = 16
COILS = 32


def plant(values, own_key, low, top_value):
    longest = values.shape.index(max(values.shape))
    spots = []
    for shift in (0, 1):
        where = [jax.random.randint(jax.random.fold_in(own_key, axis), (), 0, length) for axis, length in enumerate(values.shape)]
        where[longest] = (where[longest] + shift) % values.shape[longest]
        spots.append(tuple(where))
    return values.at[spots[0]].set(low).at[spots[1]].set(top_value)


def steps_of(own_key, dims, cuts, least, top_value):
    gain, own = 1.0, jax.random.fold_in(own_key, 6)
    for dim, parts in cuts:
        heights = jnp.exp(jax.random.uniform(jax.random.fold_in(own, dim), (parts,), jnp.float32, least / len(cuts), top_value / len(cuts)))
        gain = gain * jnp.repeat(heights, dims[dim] // parts).reshape([-1 if axis == dim else 1 for axis in range(len(dims))])
    return gain


def bell_draw(key, dims, scale, bound, pieces=(), kind=jnp.bfloat16):
    values = scale * jax.random.normal(key, dims, jnp.float32)
    if pieces:
        values = values * steps_of(key, dims, pieces, -0.22, 0.18)
    return jnp.clip(values, -bound, bound).astype(kind)


def setup_inputs(seed: int = 0) -> dict:
    arg_keys = jax.random.split(jax.random.key(seed), 9)
    return {
        "image_estimate": bell_draw(arg_keys[0], (PARTS_SIZE, NPIX, 2 * NPIX), 1.0, 6.0),
        "coil_maps": bell_draw(arg_keys[1], (COILS, NPIX, 2 * NPIX), 0.5, 3.0, ((0, 32),)),
        "field_map": jnp.clip(jax.random.uniform(arg_keys[2], (NPIX, NPIX), jnp.float32, -3.0, 3.0), -3.0, 3.0),
        "interp_rows": bell_draw(arg_keys[3], (PARTS_SIZE, SROWS, NPIX), NPIX ** -0.5, 0.3125),
        "interp_cols": bell_draw(arg_keys[4], (PARTS_SIZE, SCOLS, NPIX), NPIX ** -0.5, 0.3125),
        "measured": bell_draw(arg_keys[5], (COILS, PARTS_SIZE, SROWS, 2 * SCOLS), 1.0, 6.0, ((0, 32),)),
        "sample_time": plant(jax.random.randint(arg_keys[6], (PARTS_SIZE, SROWS), 0, (NSEG - 1) * SUBSTEPS + 1), jax.random.fold_in(arg_keys[6], 1), 0, (NSEG - 1) * SUBSTEPS).astype(jnp.int32),
        "sample_count": jax.random.randint(arg_keys[7], (PARTS_SIZE,), SROWS // 2, SROWS + 1).astype(jnp.int32),
    }


def seg_weights(sample_steps, segment):
    distance = jnp.abs(sample_steps.astype(jnp.float32) - (segment * SUBSTEPS).astype(jnp.float32)) / SUBSTEPS
    return jnp.maximum(0.0, 1.0 - distance)


def to_complex(halves):
    width = halves.shape[-1] // 2
    return halves[..., :width].astype(jnp.float32) + 1j * halves[..., width:].astype(jnp.float32)


def to_halves(values):
    return jnp.concatenate([jnp.real(values), jnp.imag(values)], axis=-1)


def reference(image_estimate, coil_maps, field_map, interp_rows, interp_cols, measured, sample_time, sample_count):
    row_ids = jnp.arange(SROWS, dtype=jnp.int32)
    factor = COILS ** -0.5
    gradients = []
    residuals = []
    for part in range(PARTS_SIZE):
        current = to_complex(image_estimate[part])
        grid_rows = interp_rows[part]
        grid_cols = interp_cols[part].astype(jnp.float32)
        sample_steps = sample_time[part]
        sampled_mask = (row_ids < sample_count[part]).astype(jnp.float32)[:, None]

        def coil_step(total, inputs):
            coil_map, coil_data = inputs
            sensitivity = to_complex(coil_map)

            def phased(segment):
                angles = field_map * (segment.astype(jnp.float32) - 0.5 * (NSEG - 1))
                return sensitivity * (jnp.cos(angles) + 1j * jnp.sin(angles))

            def forward(segment, accum):
                weighted = to_halves(current * phased(segment)).astype(jnp.bfloat16)
                rows_ft = to_halves(jnp.fft.fft(to_complex(weighted), axis=0, norm="ortho")).astype(jnp.bfloat16)
                kspace = to_halves(jnp.fft.fft(to_complex(rows_ft), axis=1, norm="ortho")).astype(jnp.bfloat16)
                picked = jnp.dot(grid_rows, kspace, preferred_element_type=jnp.float32).astype(jnp.bfloat16)
                return accum + seg_weights(sample_steps, segment)[:, None] * picked.astype(jnp.float32)

            accum = lax.fori_loop(0, NSEG, forward, jnp.zeros((SROWS, 2 * NPIX), jnp.float32))
            samples = jnp.einsum("mrn,kn->mrk", accum.reshape(SROWS, 2, NPIX), grid_cols,
                                 precision=lax.Precision.HIGHEST).reshape(SROWS, 2 * SCOLS)
            misfit = sampled_mask * (samples - coil_data.astype(jnp.float32))

            def adjoint(segment, image_sum):
                back_weighted = (seg_weights(sample_steps, segment)[:, None] * misfit).astype(jnp.bfloat16)
                spread = jnp.dot(grid_rows.T, back_weighted, preferred_element_type=jnp.float32).astype(jnp.bfloat16)
                gridded = jnp.einsum("nrk,kj->nrj", spread.reshape(NPIX, 2, SCOLS).astype(jnp.float32), grid_cols,
                                     precision=lax.Precision.HIGHEST).reshape(NPIX, 2 * NPIX).astype(jnp.bfloat16)
                back_rows = to_halves(jnp.fft.ifft(to_complex(gridded), axis=0, norm="ortho")).astype(jnp.bfloat16)
                back_image = jnp.fft.ifft(to_complex(back_rows), axis=1, norm="ortho")
                return image_sum + to_halves(jnp.conj(phased(segment)) * back_image)

            coil_image = lax.fori_loop(0, NSEG, adjoint, jnp.zeros((NPIX, 2 * NPIX), jnp.float32))
            return total + coil_image, misfit

        total, misfits = lax.scan(coil_step, jnp.zeros((NPIX, 2 * NPIX), jnp.float32),
                                  (coil_maps, measured[:, part]))
        gradients.append(factor * total)
        residuals.append(misfits)
    return jnp.stack(gradients, axis=0), jnp.stack(residuals, axis=1)
```

```python
import functools
import math

import jax
import jax.numpy as jnp
import numpy as np
from jax import lax
from jax.experimental import pallas as pl
from jax.experimental.pallas import tpu as pltpu
from jax.sharding import PartitionSpec as P

SUBSTEPS = 4
NPIX = 384
SROWS = 256
SCOLS = 128
NSEG = 16
HALF = NSEG // 2
COILS = 32
OWN_ROWS = NPIX // COILS
OWN_COLS = 2 * NPIX // NSEG
MESH = pl.DeviceIdType.MESH
F32 = jnp.float32
BF16 = jnp.bfloat16
STRIP = 16


def dft_table():
    index = np.arange(NPIX)
    angle = (index[:, None] * index[None, :] % NPIX) * (2.0 * math.pi / NPIX)
    table = np.concatenate([np.cos(angle), np.sin(angle)], 0) / math.sqrt(NPIX)
    return table.astype(np.float32)


def dot_nt(lhs, rhs):
    return lax.dot_general(lhs, rhs, (((1,), (1,)), ((), ())), preferred_element_type=F32)


def dot_nn(lhs, rhs):
    return jnp.dot(lhs, rhs, preferred_element_type=F32)


def half_angle(field):
    y = field * 0.25
    z = y * y
    sine = y * (1.0 + z * (-1.0 / 6 + z * (1.0 / 120 + z * (-1.0 / 5040 + z * (1.0 / 362880)))))
    cosine = 1.0 + z * (-0.5 + z * (1.0 / 24 + z * (-1.0 / 720 + z * (1.0 / 40320 - z * (1.0 / 3628800)))))
    return 1.0 - 2.0 * sine * sine, 2.0 * sine * cosine


def hat(steps, segment):
    return jnp.maximum(0.0, 1.0 - jnp.abs(steps - float(segment * SUBSTEPS)) * (1.0 / SUBSTEPS))


def kernel(
    image_hbm,
    maps_hbm,
    field_hbm,
    rows_hbm,
    cols_hbm,
    measured_hbm,
    time_ref,
    count_ref,
    table_hbm,
    gradient_ref,
    residual_ref,
    image,
    maps,
    field,
    rows,
    cols,
    measured,
    table,
    base_re,
    base_im,
    cos_a,
    cos_b,
    sin_a,
    sin_b,
    twice,
    lhs_a,
    lhs_b,
    mix_b,
    mix_a,
    mix_at,
    stack_p,
    stack_q,
    weight_p,
    weight_m,
    samples,
    own_coil,
    own_cos_a,
    own_cos_b,
    own_sin_a,
    own_sin_b,
    own_twice,
    turned,
    image_sum,
    outbox,
    inbox,
    load_sem,
    send_sem,
    recv_sem,
):
    seg = lax.axis_index("seg")
    coil = lax.axis_index("coil")
    block = lax.rem(seg, HALF)
    component = lax.div(seg, HALF)

    barrier = pltpu.get_barrier_semaphore()

    def greet(step, carry):
        pl.semaphore_signal(
            barrier, inc=1, device_id={"coil": lax.rem(coil + step, COILS)}, device_id_type=MESH
        )
        return carry

    loads = [
        pltpu.make_async_copy(source, target, load_sem.at[place])
        for place, (source, target) in enumerate(
            [
                (table_hbm, table),
                (cols_hbm.at[0], cols),
                (field_hbm, field),
                (image_hbm.at[0], image),
                (maps_hbm.at[0], maps),
                (rows_hbm.at[0], rows),
                (measured_hbm.at[0, 0], measured),
            ]
        )
    ]
    for load in loads:
        load.start()
    lax.fori_loop(1, COILS, greet, 0)
    for load in loads:
        load.wait()

    col_mix = dot_nt(table[...], cols[...])
    cos_mix = col_mix[:NPIX].astype(BF16)
    sin_mix = col_mix[NPIX:].astype(BF16)
    mix_b[:NPIX, :SCOLS] = cos_mix
    mix_b[:NPIX, SCOLS:] = -sin_mix
    mix_b[NPIX : 2 * NPIX, :SCOLS] = sin_mix
    mix_b[NPIX : 2 * NPIX, SCOLS:] = cos_mix
    mix_b[2 * NPIX :, :] = jnp.zeros((16, 2 * SCOLS), BF16)
    mix_a[:, :NPIX] = dot_nn(rows[...], table[:NPIX]).astype(BF16)
    mix_a[:, NPIX:] = (-dot_nn(rows[...], table[NPIX:])).astype(BF16)
    row_mix = dot_nt(table[...], rows[...])
    mix_at[:, :SROWS] = row_mix[:NPIX].astype(BF16)
    mix_at[:, SROWS:] = (-row_mix[NPIX:]).astype(BF16)

    steps = jnp.transpose(jnp.broadcast_to(time_ref[...].astype(F32), (SCOLS, SROWS)))
    for pair in range(HALF):
        upper = hat(steps, HALF + pair)
        lower = hat(steps, HALF - 1 - pair)
        weight_p[pair] = upper + lower
        weight_m[pair] = upper - lower

    for start in range(0, NPIX, STRIP):
        at = slice(start, start + STRIP)
        im_re = image[at, :NPIX].astype(F32)
        im_im = image[at, NPIX:].astype(F32)
        co_re = maps[at, :NPIX].astype(F32)
        co_im = maps[at, NPIX:].astype(F32)
        base_re[at] = im_re * co_re - im_im * co_im
        base_im[at] = im_re * co_im + im_im * co_re
        cosine, sine = half_angle(field[at])
        cos_a[at] = cosine
        cos_b[at] = cosine
        sin_a[at] = sine
        sin_b[at] = -sine
        twice[at] = 4.0 * cosine * cosine - 2.0

    width = OWN_COLS
    pick_row = lax.broadcasted_iota(jnp.int32, (2 * NPIX, 128), 0)
    pick_lane = lax.broadcasted_iota(jnp.int32, (2 * NPIX, 128), 1)
    low = pick_lane < 64
    place = jnp.where(low, pick_lane, pick_lane - 64)
    wanted = place + width * block
    real_rows = wanted + jnp.where(low, component * NPIX, (1 - component) * NPIX)
    hit = (pick_row == real_rows) & (place < width)
    sign = jnp.where(low & (component == 1), -1.0, 1.0)
    pick_coil = jnp.where(hit, sign, 0.0).astype(BF16)
    own_coil[...] = dot_nn(maps[...], pick_coil)
    pick_field = jnp.where((pick_row == wanted) & (place < width), 1.0, 0.0)[:NPIX].astype(BF16)
    whole = field[...]
    high = whole.astype(BF16)
    rest = whole - high.astype(F32)
    middle = rest.astype(BF16)
    last = (rest - middle.astype(F32)).astype(BF16)
    own_field = dot_nn(high, pick_field) + dot_nn(middle, pick_field) + dot_nn(last, pick_field)
    cosine, sine = half_angle(own_field)
    own_cos_a[...] = cosine
    own_cos_b[...] = cosine
    own_sin_a[...] = sine
    own_sin_b[...] = -sine
    own_twice[...] = 4.0 * cosine * cosine - 2.0

    def phase_image(now_cos, other_cos, now_sin, other_sin, lhs):
        for start in range(0, NPIX, STRIP):
            at = slice(start, start + STRIP)
            below = slice(NPIX + start, NPIX + start + STRIP)
            cosine = now_cos[at]
            sine = now_sin[at]
            re = base_re[at]
            im = base_im[at]
            lhs[at, :NPIX] = (re * cosine).astype(BF16)
            lhs[at, NPIX:] = (im * cosine).astype(BF16)
            lhs[below, :NPIX] = (-im * sine).astype(BF16)
            lhs[below, NPIX:] = (re * sine).astype(BF16)
            double = twice[at]
            other_cos[at] = double * cosine - other_cos[at]
            other_sin[at] = double * sine - other_sin[at]

    def add_samples(lhs, pair):
        for part, (stack, weight) in enumerate([(stack_p, weight_p), (stack_q, weight_m)]):
            grid = dot_nn(lhs[part * NPIX : (part + 1) * NPIX], mix_b[: 2 * NPIX]).astype(BF16)
            stack[:NPIX] = grid
            stack[NPIX:, :SCOLS] = -grid[:, SCOLS:]
            stack[NPIX:, SCOLS:] = grid[:, :SCOLS]
        for stack, weight in [(stack_p, weight_p), (stack_q, weight_m)]:
            scale = weight[pair]
            found = dot_nn(mix_a[...], stack[...])
            samples[...] += jnp.concatenate([scale, scale], 1) * found

    samples[...] = jnp.zeros((SROWS, 2 * SCOLS), F32)
    phase_image(cos_a, cos_b, sin_a, sin_b, lhs_a)

    def forward(step, carry):
        phase_image(cos_b, cos_a, sin_b, sin_a, lhs_b)
        add_samples(lhs_a, 2 * step)
        phase_image(cos_a, cos_b, sin_a, sin_b, lhs_a)
        add_samples(lhs_b, 2 * step + 1)
        return carry

    lax.fori_loop(0, HALF // 2, forward, 0)

    row_ids = lax.broadcasted_iota(jnp.int32, (SROWS, 2 * SCOLS), 0)
    misfit = jnp.where(row_ids < count_ref[0], samples[...] - measured[...].astype(F32), 0.0)
    samples[...] = misfit
    share = SROWS // NSEG
    residual_ref[0, 0] = samples[pl.ds(pl.multiple_of(seg * share, share), share)]

    first = pl.multiple_of(block * width, 16)
    own_mix = jnp.concatenate([mix_b[pl.ds(first, 64)], mix_b[pl.ds(first + NPIX, 64)]], 0)
    turn = dot_nt(misfit.astype(BF16), own_mix)
    lane = lax.broadcasted_iota(jnp.int32, (SROWS, 128), 1)
    swapped = pltpu.roll(turn, 64, 1)
    turned[0] = turn
    turned[1] = jnp.where(lane < 64, swapped, -swapped)
    image_sum[...] = jnp.zeros((NPIX, 128), F32)

    def add_image(pair, now_cos, other_cos, now_sin, other_sin):
        plus = weight_p[pair]
        minus = weight_m[pair]
        top = jnp.concatenate([plus * turned[0], minus * turned[1]], 1)
        bottom = jnp.concatenate([plus * turned[1], -minus * turned[0]], 1)
        spread = jnp.concatenate([top, bottom], 0).astype(BF16)
        back = dot_nn(mix_at[...], spread)
        cosine = now_cos[...]
        sine = now_sin[...]
        image_sum[...] += cosine * back[:, :128] + sine * back[:, 128:]
        other_cos[...] = own_twice[...] * cosine - other_cos[...]
        other_sin[...] = own_twice[...] * sine - other_sin[...]

    def backward(step, carry):
        add_image(2 * step, own_cos_a, own_cos_b, own_sin_a, own_sin_b)
        add_image(2 * step + 1, own_cos_b, own_cos_a, own_sin_b, own_sin_a)
        return carry

    lax.fori_loop(0, HALF // 2, backward, 0)

    tile_lane = lax.broadcasted_iota(jnp.int32, (8, 128), 1)

    def folded(tile):
        at = slice(8 * tile, 8 * tile + 8)
        value = image_sum[at] * own_coil[at]
        return value + pltpu.roll(value, 64, 1)

    for pair in range(COILS // 2):
        shared = folded(3 * pair + 1)
        outbox[2 * pair] = jnp.where(tile_lane < 64, folded(3 * pair), shared)
        outbox[2 * pair + 1] = jnp.where(tile_lane < 64, folded(3 * pair + 2), shared)

    pl.semaphore_wait(barrier, COILS - 1)

    def send(step, carry):
        target = lax.rem(coil + step, COILS)
        pltpu.make_async_remote_copy(
            src_ref=outbox.at[target],
            dst_ref=inbox.at[step - 1],
            send_sem=send_sem,
            recv_sem=recv_sem,
            device_id={"coil": target},
            device_id_type=MESH,
        ).start()
        return carry

    lax.fori_loop(1, COILS, send, 0)
    everything = pltpu.make_async_remote_copy(
        src_ref=outbox.at[pl.ds(0, COILS - 1)],
        dst_ref=inbox,
        send_sem=send_sem,
        recv_sem=recv_sem,
        device_id={"coil": lax.rem(coil + 1, COILS)},
        device_id_type=MESH,
    )
    everything.wait_recv()
    total = outbox[coil]
    for slot in range(COILS - 1):
        total = total + inbox[slot]
    total = total * (COILS ** -0.5)
    high_lanes = pltpu.roll(total, 64, 1)
    even = jnp.concatenate([total, high_lanes[:4]], 0)
    odd = jnp.concatenate([high_lanes[4:], total], 0)
    result = jnp.where(lax.rem(coil, 2) == 0, even, odd)
    gradient_ref[0] = result[:, :OWN_COLS]
    everything.wait_send()


def shards(*arguments):
    vmem = pl.BlockSpec(memory_space=pltpu.VMEM)
    anywhere = pl.BlockSpec(memory_space=pl.ANY)
    smem = pl.BlockSpec(memory_space=pltpu.SMEM)
    square = pltpu.VMEM((NPIX, NPIX), F32)
    own = pltpu.VMEM((NPIX, 128), F32)
    return tuple(
        pl.pallas_call(
            kernel,
            out_shape=(
                jax.ShapeDtypeStruct((1, OWN_ROWS, OWN_COLS), F32),
                jax.ShapeDtypeStruct((1, 1, SROWS // NSEG, 2 * SCOLS), F32),
            ),
            in_specs=[anywhere] * 6 + [vmem, smem, anywhere],
            out_specs=(vmem, vmem),
            scratch_shapes=[
                pltpu.VMEM((NPIX, 2 * NPIX), BF16),
                pltpu.VMEM((NPIX, 2 * NPIX), BF16),
                square,
                pltpu.VMEM((SROWS, NPIX), BF16),
                pltpu.VMEM((SCOLS, NPIX), BF16),
                pltpu.VMEM((SROWS, 2 * SCOLS), BF16),
                pltpu.VMEM((2 * NPIX, NPIX), BF16),
                square,
                square,
                square,
                square,
                square,
                square,
                square,
                pltpu.VMEM((2 * NPIX, 2 * NPIX), BF16),
                pltpu.VMEM((2 * NPIX, 2 * NPIX), BF16),
                pltpu.VMEM((2 * NPIX + 16, 2 * SCOLS), BF16),
                pltpu.VMEM((SROWS, 2 * NPIX), BF16),
                pltpu.VMEM((NPIX, 2 * SROWS), BF16),
                pltpu.VMEM((2 * NPIX, 2 * SCOLS), BF16),
                pltpu.VMEM((2 * NPIX, 2 * SCOLS), BF16),
                pltpu.VMEM((HALF, SROWS, SCOLS), F32),
                pltpu.VMEM((HALF, SROWS, SCOLS), F32),
                pltpu.VMEM((SROWS, 2 * SCOLS), F32),
                own,
                own,
                own,
                own,
                own,
                own,
                pltpu.VMEM((2, SROWS, 128), F32),
                own,
                pltpu.VMEM((COILS, 8, 128), F32),
                pltpu.VMEM((COILS - 1, 8, 128), F32),
                pltpu.SemaphoreType.DMA((7,)),
                pltpu.SemaphoreType.DMA,
                pltpu.SemaphoreType.DMA,
            ],
            compiler_params=pltpu.CompilerParams(
                collective_id=0, has_side_effects=True, vmem_limit_bytes=48 * 2**20
            ),
        )(*arguments, jnp.asarray(dft_table()).astype(BF16))
    )


def solution(mesh):
    in_specs = (P(), P("coil", None, None), P(), P(), P(), P("coil", None, None, None), P(), P())
    out_specs = (P(None, "coil", "seg"), P("coil", None, "seg", None))
    return jax.shard_map(shards, mesh=mesh, in_specs=in_specs, out_specs=out_specs, check_vma=False)
```

```python
import functools
import math

import jax
import jax.numpy as jnp
import numpy as np
from jax import lax
from jax.experimental import pallas as pl
from jax.experimental.pallas import tpu as pltpu
from jax.sharding import PartitionSpec as P

SUBSTEPS = 4
NPIX = 384
SROWS = 256
SCOLS = 128
NSEG = 16
HALF = NSEG // 2
COILS = 32
OWN_ROWS = NPIX // COILS
OWN_COLS = 2 * NPIX // NSEG
MESH = pl.DeviceIdType.MESH
F32 = jnp.float32
BF16 = jnp.bfloat16
STRIP = 16
GROUP = 1


def dft_table():
    index = np.arange(NPIX)
    angle = (index[:, None] * index[None, :] % NPIX) * (2.0 * math.pi / NPIX)
    table = np.concatenate([np.cos(angle), np.sin(angle)], 0) / math.sqrt(NPIX)
    return table.astype(np.float32)


def dot_nt(lhs, rhs):
    return lax.dot_general(lhs, rhs, (((1,), (1,)), ((), ())), preferred_element_type=F32)


def dot_nn(lhs, rhs):
    return jnp.dot(lhs, rhs, preferred_element_type=F32)


def half_angle(field):
    y = field * 0.25
    z = y * y
    sine = y * (1.0 + z * (-1.0 / 6 + z * (1.0 / 120 + z * (-1.0 / 5040 + z * (1.0 / 362880)))))
    cosine = 1.0 + z * (-0.5 + z * (1.0 / 24 + z * (-1.0 / 720 + z * (1.0 / 40320 - z * (1.0 / 3628800)))))
    return 1.0 - 2.0 * sine * sine, 2.0 * sine * cosine


def hat(steps, segment):
    return jnp.maximum(0.0, 1.0 - jnp.abs(steps - float(segment * SUBSTEPS)) * (1.0 / SUBSTEPS))


def kernel(
    image_hbm,
    maps_hbm,
    field_hbm,
    rows_hbm,
    cols_hbm,
    measured_hbm,
    time_hbm,
    count_hbm,
    table_hbm,
    gradient_ref,
    residual_ref,
    image,
    maps,
    field,
    rows,
    cols,
    measured,
    table,
    time_ref,
    count_ref,
    base_re,
    base_im,
    cos_a,
    cos_b,
    sin_a,
    sin_b,
    twice,
    lhs_a,
    lhs_b,
    mix_b,
    mix_a,
    mix_at,
    grid_a,
    grid_b,
    quarters,
    weight_p,
    weight_m,
    samples,
    own_coil,
    own_cos_a,
    own_cos_b,
    own_sin_a,
    own_sin_b,
    own_twice,
    turned,
    image_sum,
    outbox,
    inbox,
    load_sem,
    send_sem,
    recv_sem,
):
    seg = lax.axis_index("seg")
    coil = lax.axis_index("coil")
    block = lax.rem(seg, HALF)
    component = lax.div(seg, HALF)

    barrier = pltpu.get_barrier_semaphore()

    def greet(step, carry):
        pl.semaphore_signal(
            barrier, inc=1, device_id={"coil": lax.rem(coil + step, COILS)}, device_id_type=MESH
        )
        return carry

    pairs = [
        (table_hbm, table),
        (cols_hbm.at[0], cols),
        (rows_hbm.at[0], rows),
        (time_hbm, time_ref),
        (field_hbm, field),
        (image_hbm.at[0], image),
        (maps_hbm.at[0], maps),
        (measured_hbm.at[0, 0], measured),
        (count_hbm, count_ref),
    ]
    loads = [
        pltpu.make_async_copy(source, target, load_sem.at[place])
        for place, (source, target) in enumerate(pairs)
    ]
    for load in loads:
        load.start()
    lax.fori_loop(1, COILS, greet, 0)
    for load in loads[:5]:
        load.wait()

    col_mix = dot_nt(table[...], cols[...])
    cos_mix = col_mix[:NPIX].astype(BF16)
    sin_mix = col_mix[NPIX:].astype(BF16)
    mix_b[:NPIX, :SCOLS] = cos_mix
    mix_b[:NPIX, SCOLS:] = -sin_mix
    mix_b[NPIX : 2 * NPIX, :SCOLS] = sin_mix
    mix_b[NPIX : 2 * NPIX, SCOLS:] = cos_mix
    mix_b[2 * NPIX :, :] = jnp.zeros((16, 2 * SCOLS), BF16)
    mix_a[:SROWS] = dot_nn(rows[...], table[:NPIX]).astype(BF16)
    mix_a[SROWS:] = (-dot_nn(rows[...], table[NPIX:])).astype(BF16)
    row_mix = dot_nt(table[...], rows[...])
    mix_at[:, :SROWS] = row_mix[:NPIX].astype(BF16)
    mix_at[:, SROWS:] = (-row_mix[NPIX:]).astype(BF16)

    steps = jnp.transpose(jnp.broadcast_to(time_ref[...].astype(F32), (SCOLS, SROWS)))
    for pair in range(HALF):
        upper = hat(steps, HALF + pair)
        lower = hat(steps, HALF - 1 - pair)
        weight_p[pair] = upper + lower
        weight_m[pair] = upper - lower

    for start in range(0, NPIX, STRIP):
        at = slice(start, start + STRIP)
        cosine, sine = half_angle(field[at])
        cos_a[at] = cosine
        cos_b[at] = cosine
        sin_a[at] = sine
        sin_b[at] = -sine
        twice[at] = 4.0 * cosine * cosine - 2.0

    width = OWN_COLS
    near = lax.div(block * width, 128)
    near_lane = pl.multiple_of(near * 128, 128)
    far_lane = pl.multiple_of(jnp.minimum(near + 1, NPIX // 128 - 1) * 128, 128)
    offset = block * width - near_lane
    back_turn = lax.rem(128 - offset, 128)
    whole_lane = lax.broadcasted_iota(jnp.int32, (NPIX, 128), 1)
    unbroken = whole_lane < 128 - offset

    def own_columns(near_half, far_half):
        return jnp.where(unbroken, pltpu.roll(near_half, back_turn, 1), pltpu.roll(far_half, back_turn, 1))

    def doubled(low, high):
        return jnp.where(whole_lane < 64, low, pltpu.roll(high, 64, 1))

    own_field = own_columns(field[:, pl.ds(near_lane, 128)], field[:, pl.ds(far_lane, 128)])
    own_field = doubled(own_field, own_field)
    cosine, sine = half_angle(own_field)
    own_cos_a[...] = cosine
    own_cos_b[...] = cosine
    own_sin_a[...] = sine
    own_sin_b[...] = -sine
    own_twice[...] = 4.0 * cosine * cosine - 2.0

    for load in loads[5:7]:
        load.wait()
    for start in range(0, NPIX, STRIP):
        at = slice(start, start + STRIP)
        im_re = image[at, :NPIX].astype(F32)
        im_im = image[at, NPIX:].astype(F32)
        co_re = maps[at, :NPIX].astype(F32)
        co_im = maps[at, NPIX:].astype(F32)
        base_re[at] = (im_re * co_re - im_im * co_im).astype(BF16)
        base_im[at] = (im_re * co_im + im_im * co_re).astype(BF16)

    def own_map(start):
        halves = [
            maps[:, pl.ds(pl.multiple_of(start + lane, 128), 128)].astype(F32)
            for lane in (near_lane, far_lane)
        ]
        return own_columns(*halves)

    map_re, map_im = own_map(0), own_map(NPIX)
    own_coil[...] = jnp.where(component == 0, doubled(map_re, map_im), doubled(-map_im, map_re))

    def phase_image(lhs):
        for start in range(0, NPIX, STRIP):
            at = slice(start, start + STRIP)
            re = base_re[at]
            im = base_im[at]
            double = twice[at]
            cosine, sine = cos_a[at], sin_a[at]
            last_cosine, last_sine = cos_b[at], sin_b[at]
            for pair in range(GROUP):
                plain = slice(2 * pair * NPIX + start, 2 * pair * NPIX + start + STRIP)
                below = slice(plain.start + NPIX, plain.stop + NPIX)
                short_cosine = cosine.astype(BF16)
                short_sine = sine.astype(BF16)
                lhs[plain, :NPIX] = re * short_cosine
                lhs[plain, NPIX:] = im * short_cosine
                lhs[below, :NPIX] = -im * short_sine
                lhs[below, NPIX:] = re * short_sine
                cosine, last_cosine = double * cosine - last_cosine, cosine
                sine, last_sine = double * sine - last_sine, sine
            cos_a[at], sin_a[at] = cosine, sine
            cos_b[at], sin_b[at] = last_cosine, last_sine

    def transform(lhs, grid):
        grid[...] = dot_nn(lhs[...], mix_b[: 2 * NPIX]).astype(BF16)

    def add_samples(grid, first):
        scales = []
        for pair in range(GROUP):
            for weight in (weight_p, weight_m):
                short = weight[first + pair].astype(BF16)
                scales.append(jnp.concatenate([jnp.concatenate([short] * 3, 1)] * 2, 0) * mix_a[...])
        quarters[...] += dot_nn(jnp.concatenate(scales, 1), grid[...])

    quarters[...] = jnp.zeros((2 * SROWS, 2 * SCOLS), F32)
    groups = HALF // GROUP
    both_lhs, both_grids = (lhs_a, lhs_b), (grid_a, grid_b)
    for step in range(groups + 2):
        if step < groups:
            phase_image(both_lhs[step % 2])
        if 0 < step <= groups:
            transform(both_lhs[(step - 1) % 2], both_grids[(step - 1) % 2])
        if step > 1:
            add_samples(both_grids[step % 2], (step - 2) * GROUP)
    top, bottom = quarters[:SROWS], quarters[SROWS:]
    samples[:, :SCOLS] = top[:, :SCOLS] - bottom[:, SCOLS:]
    samples[:, SCOLS:] = top[:, SCOLS:] + bottom[:, :SCOLS]

    for load in loads[7:]:
        load.wait()
    row_ids = lax.broadcasted_iota(jnp.int32, (SROWS, 2 * SCOLS), 0)
    misfit = jnp.where(row_ids < count_ref[0], samples[...] - measured[...].astype(F32), 0.0)
    samples[...] = misfit
    share = SROWS // NSEG
    residual_ref[0, 0] = samples[pl.ds(pl.multiple_of(seg * share, share), share)]

    first = pl.multiple_of(block * width, 16)
    own_mix = jnp.concatenate([mix_b[pl.ds(first, 64)], mix_b[pl.ds(first + NPIX, 64)]], 0)
    turn = dot_nt(misfit.astype(BF16), own_mix)
    lane = lax.broadcasted_iota(jnp.int32, (SROWS, 128), 1)
    swapped = pltpu.roll(turn, 64, 1)
    turned[0] = turn
    turned[1] = jnp.where(lane < 64, swapped, -swapped)
    image_sum[...] = jnp.zeros((NPIX, 128), F32)

    def add_image(pair, now_cos, other_cos, now_sin, other_sin):
        plus = weight_p[pair]
        minus = weight_m[pair]
        top = jnp.concatenate([plus * turned[0], minus * turned[1]], 1)
        bottom = jnp.concatenate([plus * turned[1], -minus * turned[0]], 1)
        spread = jnp.concatenate([top, bottom], 0).astype(BF16)
        back = dot_nn(mix_at[...], spread)
        cosine = now_cos[...]
        sine = now_sin[...]
        image_sum[...] += cosine * back[:, :128] + sine * back[:, 128:]
        other_cos[...] = own_twice[...] * cosine - other_cos[...]
        other_sin[...] = own_twice[...] * sine - other_sin[...]

    for pair in range(HALF):
        if pair % 2 == 0:
            add_image(pair, own_cos_a, own_cos_b, own_sin_a, own_sin_b)
        else:
            add_image(pair, own_cos_b, own_cos_a, own_sin_b, own_sin_a)

    value = image_sum[...] * own_coil[...]
    image_sum[...] = value + pltpu.roll(value, 64, 1)
    half = OWN_ROWS // 2
    tile_lane = lax.broadcasted_iota(jnp.int32, (half, 128), 1)
    for target in range(COILS):
        first_row = target * OWN_ROWS
        outbox[target] = jnp.where(
            tile_lane < 64,
            image_sum[first_row : first_row + half],
            image_sum[first_row + half : first_row + OWN_ROWS],
        )

    pl.semaphore_wait(barrier, COILS - 1)

    def send(step, carry):
        target = lax.rem(coil + step, COILS)
        pltpu.make_async_remote_copy(
            src_ref=outbox.at[target],
            dst_ref=inbox.at[step - 1],
            send_sem=send_sem,
            recv_sem=recv_sem,
            device_id={"coil": target},
            device_id_type=MESH,
        ).start()
        return carry

    lax.fori_loop(1, COILS, send, 0)
    everything = pltpu.make_async_remote_copy(
        src_ref=outbox.at[pl.ds(0, COILS - 1)],
        dst_ref=inbox,
        send_sem=send_sem,
        recv_sem=recv_sem,
        device_id={"coil": lax.rem(coil + 1, COILS)},
        device_id_type=MESH,
    )
    everything.wait_recv()
    total = outbox[coil]
    for slot in range(COILS - 1):
        total = total + inbox[slot]
    total = total * (COILS ** -0.5)
    gradient_ref[0, :half] = total[:, :OWN_COLS]
    gradient_ref[0, half:] = pltpu.roll(total, 64, 1)[:, :OWN_COLS]
    everything.wait_send()


def shards(*arguments):
    vmem = pl.BlockSpec(memory_space=pltpu.VMEM)
    anywhere = pl.BlockSpec(memory_space=pl.ANY)
    square = pltpu.VMEM((NPIX, NPIX), F32)
    own = pltpu.VMEM((NPIX, 128), F32)
    return tuple(
        pl.pallas_call(
            kernel,
            out_shape=(
                jax.ShapeDtypeStruct((1, OWN_ROWS, OWN_COLS), F32),
                jax.ShapeDtypeStruct((1, 1, SROWS // NSEG, 2 * SCOLS), F32),
            ),
            in_specs=[anywhere] * 9,
            out_specs=(vmem, vmem),
            scratch_shapes=[
                pltpu.VMEM((NPIX, 2 * NPIX), BF16),
                pltpu.VMEM((NPIX, 2 * NPIX), BF16),
                square,
                pltpu.VMEM((SROWS, NPIX), BF16),
                pltpu.VMEM((SCOLS, NPIX), BF16),
                pltpu.VMEM((SROWS, 2 * SCOLS), BF16),
                pltpu.VMEM((2 * NPIX, NPIX), BF16),
                pltpu.VMEM((1, SROWS), jnp.int32),
                pltpu.SMEM((1,), jnp.int32),
                pltpu.VMEM((NPIX, NPIX), BF16),
                pltpu.VMEM((NPIX, NPIX), BF16),
                square,
                square,
                square,
                square,
                square,
                pltpu.VMEM((2 * GROUP * NPIX, 2 * NPIX), BF16),
                pltpu.VMEM((2 * GROUP * NPIX, 2 * NPIX), BF16),
                pltpu.VMEM((2 * NPIX + 16, 2 * SCOLS), BF16),
                pltpu.VMEM((2 * SROWS, NPIX), BF16),
                pltpu.VMEM((NPIX, 2 * SROWS), BF16),
                pltpu.VMEM((2 * GROUP * NPIX, 2 * SCOLS), BF16),
                pltpu.VMEM((2 * GROUP * NPIX, 2 * SCOLS), BF16),
                pltpu.VMEM((2 * SROWS, 2 * SCOLS), F32),
                pltpu.VMEM((HALF, SROWS, SCOLS), F32),
                pltpu.VMEM((HALF, SROWS, SCOLS), F32),
                pltpu.VMEM((SROWS, 2 * SCOLS), F32),
                own,
                own,
                own,
                own,
                own,
                own,
                pltpu.VMEM((2, SROWS, 128), F32),
                own,
                pltpu.VMEM((COILS, OWN_ROWS // 2, 128), F32),
                pltpu.VMEM((COILS - 1, OWN_ROWS // 2, 128), F32),
                pltpu.SemaphoreType.DMA((9,)),
                pltpu.SemaphoreType.DMA,
                pltpu.SemaphoreType.DMA,
            ],
            compiler_params=pltpu.CompilerParams(
                collective_id=0, has_side_effects=True, vmem_limit_bytes=60 * 2**20
            ),
        )(*arguments, jnp.asarray(dft_table()).astype(BF16))
    )


def solution(mesh):
    in_specs = (P(), P("coil", None, None), P(), P(), P(), P("coil", None, None, None), P(), P())
    out_specs = (P(None, "coil", "seg"), P("coil", None, "seg", None))
    return jax.shard_map(shards, mesh=mesh, in_specs=in_specs, out_specs=out_specs, check_vma=False)
```

```python
import functools
import math

import jax
import jax.numpy as jnp
import numpy as np
from jax import lax
from jax.experimental import pallas as pl
from jax.experimental.pallas import tpu as pltpu
from jax.sharding import PartitionSpec as P

SUBSTEPS = 4
NPIX = 384
SROWS = 256
SCOLS = 128
NSEG = 16
HALF = NSEG // 2
COILS = 32
OWN_ROWS = NPIX // COILS
OWN_COLS = 2 * NPIX // NSEG
MESH = pl.DeviceIdType.MESH
F32 = jnp.float32
BF16 = jnp.bfloat16
STRIP = 16
SPLIT = 1
LOADS = 5 + 4 * SPLIT


def dft_table():
    index = np.arange(NPIX)
    angle = (index[:, None] * index[None, :] % NPIX) * (2.0 * math.pi / NPIX)
    table = np.concatenate([np.cos(angle), np.sin(angle)], 0) / math.sqrt(NPIX)
    return table.astype(np.float32)


def dot_nt(lhs, rhs):
    return lax.dot_general(lhs, rhs, (((1,), (1,)), ((), ())), preferred_element_type=F32)


def dot_nn(lhs, rhs):
    return jnp.dot(lhs, rhs, preferred_element_type=F32)


def half_angle(field):
    y = field * 0.25
    z = y * y
    sine = y * (1.0 + z * (-1.0 / 6 + z * (1.0 / 120 + z * (-1.0 / 5040 + z * (1.0 / 362880)))))
    cosine = 1.0 + z * (-0.5 + z * (1.0 / 24 + z * (-1.0 / 720 + z * (1.0 / 40320 - z * (1.0 / 3628800)))))
    return 1.0 - 2.0 * sine * sine, 2.0 * sine * cosine


def hat(steps, segment):
    return jnp.maximum(0.0, 1.0 - jnp.abs(steps - float(segment * SUBSTEPS)) * (1.0 / SUBSTEPS))


def kernel(
    image_hbm,
    maps_hbm,
    field_hbm,
    rows_hbm,
    cols_hbm,
    measured_hbm,
    time_hbm,
    count_hbm,
    table_hbm,
    gradient_ref,
    residual_ref,
    image,
    maps,
    field,
    rows,
    cols,
    measured,
    table,
    time_ref,
    count_ref,
    base_re,
    base_im,
    cos_a,
    cos_b,
    sin_a,
    sin_b,
    twice,
    lhs_a,
    lhs_b,
    mix_b,
    mix_a,
    mix_at,
    grid_a,
    grid_b,
    quarters,
    weight_p,
    weight_m,
    samples,
    own_coil,
    own_cos_a,
    own_cos_b,
    own_sin_a,
    own_sin_b,
    own_twice,
    turned,
    spread,
    image_sum,
    outbox,
    inbox,
    load_sem,
    send_sem,
    recv_sem,
):
    seg = lax.axis_index("seg")
    coil = lax.axis_index("coil")
    block = lax.rem(seg, HALF)
    component = lax.div(seg, HALF)

    barrier = pltpu.get_barrier_semaphore()

    def greet(step, carry):
        pl.semaphore_signal(
            barrier, inc=1, device_id={"coil": lax.rem(coil + step, COILS)}, device_id_type=MESH
        )
        return carry

    stages = [
        [(table_hbm, table, 2 * NPIX), (cols_hbm.at[0], cols, 0), (rows_hbm.at[0], rows, 0)],
        [(time_hbm, time_ref, 0), (field_hbm, field, NPIX)],
        [(image_hbm.at[0], image, NPIX), (maps_hbm.at[0], maps, NPIX)],
        [(measured_hbm.at[0, 0], measured, 0), (count_hbm, count_ref, 0)],
    ]
    loads = []
    places = iter(range(LOADS))
    for stage in stages:
        loads.append([])
        for source, target, length in stage:
            pieces = [(source, target)]
            if length:
                piece = length // SPLIT
                pieces = [
                    (source.at[pl.ds(start, piece)], target.at[pl.ds(start, piece)])
                    for start in range(0, length, piece)
                ]
            for piece_source, piece_target in pieces:
                copy = pltpu.make_async_copy(piece_source, piece_target, load_sem.at[next(places)])
                copy.start()
                loads[-1].append(copy)
    lax.fori_loop(1, COILS, greet, 0)

    def arrived(stage):
        for copy in loads[stage]:
            copy.wait()

    arrived(0)
    col_mix = dot_nt(table[...], cols[...])
    cos_mix = col_mix[:NPIX].astype(BF16)
    sin_mix = col_mix[NPIX:].astype(BF16)
    mix_b[:NPIX, :SCOLS] = cos_mix
    mix_b[:NPIX, SCOLS:] = -sin_mix
    mix_b[NPIX : 2 * NPIX, :SCOLS] = sin_mix
    mix_b[NPIX : 2 * NPIX, SCOLS:] = cos_mix
    mix_b[2 * NPIX :, :] = jnp.zeros((16, 2 * SCOLS), BF16)
    mix_a[:SROWS] = dot_nn(rows[...], table[:NPIX]).astype(BF16)
    mix_a[SROWS:] = (-dot_nn(rows[...], table[NPIX:])).astype(BF16)
    row_mix = dot_nt(table[...], rows[...])
    mix_at[:, :SROWS] = row_mix[:NPIX].astype(BF16)
    mix_at[:, SROWS:] = (-row_mix[NPIX:]).astype(BF16)

    arrived(1)

    steps = jnp.transpose(jnp.broadcast_to(time_ref[...].astype(F32), (SCOLS, SROWS)))
    for pair in range(HALF):
        upper = hat(steps, HALF + pair)
        lower = hat(steps, HALF - 1 - pair)
        weight_p[pair] = upper + lower
        weight_m[pair] = upper - lower

    for start in range(0, NPIX, STRIP):
        at = slice(start, start + STRIP)
        cosine, sine = half_angle(field[at])
        cos_a[at] = cosine
        cos_b[at] = cosine
        sin_a[at] = sine
        sin_b[at] = -sine
        twice[at] = 4.0 * cosine * cosine - 2.0

    width = OWN_COLS
    near = lax.div(block * width, 128)
    near_lane = pl.multiple_of(near * 128, 128)
    far_lane = pl.multiple_of(jnp.minimum(near + 1, NPIX // 128 - 1) * 128, 128)
    offset = block * width - near_lane
    back_turn = lax.rem(128 - offset, 128)
    whole_lane = lax.broadcasted_iota(jnp.int32, (NPIX, 128), 1)
    unbroken = whole_lane < 128 - offset

    def own_columns(near_half, far_half):
        return jnp.where(unbroken, pltpu.roll(near_half, back_turn, 1), pltpu.roll(far_half, back_turn, 1))

    def doubled(low, high):
        return jnp.where(whole_lane < 64, low, pltpu.roll(high, 64, 1))

    own_field = own_columns(field[:, pl.ds(near_lane, 128)], field[:, pl.ds(far_lane, 128)])
    own_field = doubled(own_field, own_field)
    cosine, sine = half_angle(own_field)
    own_cos_a[...] = cosine
    own_cos_b[...] = cosine
    own_sin_a[...] = sine
    own_sin_b[...] = -sine
    own_twice[...] = 4.0 * cosine * cosine - 2.0

    arrived(2)
    for start in range(0, NPIX, STRIP):
        at = slice(start, start + STRIP)
        im_re = image[at, :NPIX].astype(F32)
        im_im = image[at, NPIX:].astype(F32)
        co_re = maps[at, :NPIX].astype(F32)
        co_im = maps[at, NPIX:].astype(F32)
        base_re[at] = (im_re * co_re - im_im * co_im).astype(BF16)
        base_im[at] = (im_re * co_im + im_im * co_re).astype(BF16)

    def own_map(start):
        halves = [
            maps[:, pl.ds(pl.multiple_of(start + lane, 128), 128)].astype(F32)
            for lane in (near_lane, far_lane)
        ]
        return own_columns(*halves)

    map_re, map_im = own_map(0), own_map(NPIX)
    own_coil[...] = jnp.where(component == 0, doubled(map_re, map_im), doubled(-map_im, map_re))

    def phase_image(lhs, now_cos, other_cos, now_sin, other_sin):
        for start in range(0, NPIX, STRIP):
            at = slice(start, start + STRIP)
            below = slice(NPIX + start, NPIX + start + STRIP)
            re = base_re[at]
            im = base_im[at]
            cosine, sine = now_cos[at], now_sin[at]
            short_cosine = cosine.astype(BF16)
            short_sine = sine.astype(BF16)
            lhs[at, :NPIX] = re * short_cosine
            lhs[at, NPIX:] = im * short_cosine
            lhs[below, :NPIX] = -im * short_sine
            lhs[below, NPIX:] = re * short_sine
            double = twice[at]
            other_cos[at] = double * cosine - other_cos[at]
            other_sin[at] = double * sine - other_sin[at]

    def transform(lhs, grid):
        grid[...] = dot_nn(lhs[...], mix_b[: 2 * NPIX]).astype(BF16)

    def add_samples(grid, pair):
        scales = []
        for weight in (weight_p, weight_m):
            short = weight[pair].astype(BF16)
            scales.append(jnp.concatenate([jnp.concatenate([short] * 3, 1)] * 2, 0) * mix_a[...])
        quarters[...] += dot_nn(jnp.concatenate(scales, 1), grid[...])

    quarters[...] = jnp.zeros((2 * SROWS, 2 * SCOLS), F32)
    both_lhs, both_grids = (lhs_a, lhs_b), (grid_a, grid_b)
    for step in range(HALF + 2):
        if step < HALF:
            if step % 2 == 0:
                phase_image(lhs_a, cos_a, cos_b, sin_a, sin_b)
            else:
                phase_image(lhs_b, cos_b, cos_a, sin_b, sin_a)
        if 0 < step <= HALF:
            transform(both_lhs[(step - 1) % 2], both_grids[(step - 1) % 2])
        if step > 1:
            add_samples(both_grids[step % 2], step - 2)
    top, bottom = quarters[:SROWS], quarters[SROWS:]
    samples[:, :SCOLS] = top[:, :SCOLS] - bottom[:, SCOLS:]
    samples[:, SCOLS:] = top[:, SCOLS:] + bottom[:, :SCOLS]

    arrived(3)
    row_ids = lax.broadcasted_iota(jnp.int32, (SROWS, 2 * SCOLS), 0)
    misfit = jnp.where(row_ids < count_ref[0], samples[...] - measured[...].astype(F32), 0.0)
    samples[...] = misfit
    share = SROWS // NSEG
    residual_ref[0, 0] = samples[pl.ds(pl.multiple_of(seg * share, share), share)]

    first = pl.multiple_of(block * width, 16)
    own_mix = jnp.concatenate([mix_b[pl.ds(first, 64)], mix_b[pl.ds(first + NPIX, 64)]], 0)
    turn = dot_nt(misfit.astype(BF16), own_mix)
    lane = lax.broadcasted_iota(jnp.int32, (SROWS, 128), 1)
    swapped = pltpu.roll(turn, 64, 1)
    turned[0] = turn
    turned[1] = jnp.where(lane < 64, swapped, -swapped)
    for pair in range(HALF):
        plus = weight_p[pair]
        minus = weight_m[pair]
        spread[pair, :SROWS, :128] = (plus * turned[0]).astype(BF16)
        spread[pair, :SROWS, 128:] = (minus * turned[1]).astype(BF16)
        spread[pair, SROWS:, :128] = (plus * turned[1]).astype(BF16)
        spread[pair, SROWS:, 128:] = (-minus * turned[0]).astype(BF16)

    rows_half = NPIX // 2
    coils_half = COILS // 2
    half = OWN_ROWS // 2
    lanes = lax.broadcasted_iota(jnp.int32, (half, 128), 1)
    own_half = lax.div(coil, coils_half)

    def make_tiles(which):
        at = pl.ds(pl.multiple_of(which * rows_half, rows_half), rows_half)
        cosine, sine = own_cos_a[at], own_sin_a[at]
        last_cosine, last_sine = own_cos_b[at], own_sin_b[at]
        double = own_twice[at]
        for pair in range(HALF):
            back = dot_nn(mix_at[at], spread[pair])
            term = cosine * back[:, :128] + sine * back[:, 128:]
            image_sum[...] = term if pair == 0 else image_sum[...] + term
            cosine, last_cosine = double * cosine - last_cosine, cosine
            sine, last_sine = double * sine - last_sine, sine
        value = image_sum[...] * own_coil[at]
        image_sum[...] = value + pltpu.roll(value, 64, 1)
        for place in range(coils_half):
            first_row = place * OWN_ROWS
            outbox[which * coils_half + place] = jnp.where(
                lanes < 64,
                image_sum[first_row : first_row + half],
                image_sum[first_row + half : first_row + OWN_ROWS],
            )

    def send(which, first):
        for step in range(first, coils_half):
            target = which * coils_half + lax.rem(coil + step, coils_half)
            pltpu.make_async_remote_copy(
                src_ref=outbox.at[target],
                dst_ref=inbox.at[coil],
                send_sem=send_sem,
                recv_sem=recv_sem,
                device_id={"coil": target},
                device_id_type=MESH,
            ).start()

    make_tiles(1 - own_half)
    pl.semaphore_wait(barrier, COILS - 1)
    send(1 - own_half, 0)
    make_tiles(own_half)
    send(own_half, 1)
    inbox[coil] = outbox[coil]
    everything = pltpu.make_async_remote_copy(
        src_ref=outbox.at[pl.ds(0, COILS - 1)],
        dst_ref=inbox.at[pl.ds(0, COILS - 1)],
        send_sem=send_sem,
        recv_sem=recv_sem,
        device_id={"coil": lax.rem(coil + 1, COILS)},
        device_id_type=MESH,
    )
    everything.wait_recv()
    total = inbox[0]
    for slot in range(1, COILS):
        total = total + inbox[slot]
    total = total * (COILS ** -0.5)
    gradient_ref[0, :half] = total[:, :OWN_COLS]
    gradient_ref[0, half:] = pltpu.roll(total, 64, 1)[:, :OWN_COLS]
    everything.wait_send()


def shards(*arguments):
    vmem = pl.BlockSpec(memory_space=pltpu.VMEM)
    anywhere = pl.BlockSpec(memory_space=pl.ANY)
    square = pltpu.VMEM((NPIX, NPIX), F32)
    own = pltpu.VMEM((NPIX, 128), F32)
    return tuple(
        pl.pallas_call(
            kernel,
            out_shape=(
                jax.ShapeDtypeStruct((1, OWN_ROWS, OWN_COLS), F32),
                jax.ShapeDtypeStruct((1, 1, SROWS // NSEG, 2 * SCOLS), F32),
            ),
            in_specs=[anywhere] * 9,
            out_specs=(vmem, vmem),
            scratch_shapes=[
                pltpu.VMEM((NPIX, 2 * NPIX), BF16),
                pltpu.VMEM((NPIX, 2 * NPIX), BF16),
                square,
                pltpu.VMEM((SROWS, NPIX), BF16),
                pltpu.VMEM((SCOLS, NPIX), BF16),
                pltpu.VMEM((SROWS, 2 * SCOLS), BF16),
                pltpu.VMEM((2 * NPIX, NPIX), BF16),
                pltpu.VMEM((1, SROWS), jnp.int32),
                pltpu.SMEM((1,), jnp.int32),
                pltpu.VMEM((NPIX, NPIX), BF16),
                pltpu.VMEM((NPIX, NPIX), BF16),
                square,
                square,
                square,
                square,
                square,
                pltpu.VMEM((2 * NPIX, 2 * NPIX), BF16),
                pltpu.VMEM((2 * NPIX, 2 * NPIX), BF16),
                pltpu.VMEM((2 * NPIX + 16, 2 * SCOLS), BF16),
                pltpu.VMEM((2 * SROWS, NPIX), BF16),
                pltpu.VMEM((NPIX, 2 * SROWS), BF16),
                pltpu.VMEM((2 * NPIX, 2 * SCOLS), BF16),
                pltpu.VMEM((2 * NPIX, 2 * SCOLS), BF16),
                pltpu.VMEM((2 * SROWS, 2 * SCOLS), F32),
                pltpu.VMEM((HALF, SROWS, SCOLS), F32),
                pltpu.VMEM((HALF, SROWS, SCOLS), F32),
                pltpu.VMEM((SROWS, 2 * SCOLS), F32),
                own,
                own,
                own,
                own,
                own,
                own,
                pltpu.VMEM((2, SROWS, 128), F32),
                pltpu.VMEM((HALF, 2 * SROWS, 2 * 128), BF16),
                pltpu.VMEM((NPIX // 2, 128), F32),
                pltpu.VMEM((COILS, OWN_ROWS // 2, 128), F32),
                pltpu.VMEM((COILS, OWN_ROWS // 2, 128), F32),
                pltpu.SemaphoreType.DMA((LOADS,)),
                pltpu.SemaphoreType.DMA,
                pltpu.SemaphoreType.DMA,
            ],
            compiler_params=pltpu.CompilerParams(
                collective_id=0, has_side_effects=True, vmem_limit_bytes=60 * 2**20
            ),
        )(*arguments, jnp.asarray(dft_table()).astype(BF16))
    )


def solution(mesh):
    in_specs = (P(), P("coil", None, None), P(), P(), P(), P("coil", None, None, None), P(), P())
    out_specs = (P(None, "coil", "seg"), P("coil", None, "seg", None))
    return jax.shard_map(shards, mesh=mesh, in_specs=in_specs, out_specs=out_specs, check_vma=False)
```

```python
import functools
import math

import jax
import jax.numpy as jnp
import numpy as np
from jax import lax
from jax.experimental import pallas as pl
from jax.experimental.pallas import tpu as pltpu
from jax.sharding import PartitionSpec as P

SUBSTEPS = 4
NPIX = 384
SROWS = 256
SCOLS = 128
NSEG = 16
HALF = NSEG // 2
COILS = 32
OWN_ROWS = NPIX // COILS
OWN_COLS = 2 * NPIX // NSEG
MESH = pl.DeviceIdType.MESH
F32 = jnp.float32
BF16 = jnp.bfloat16
STRIP = 16
BAND = 128
BANDS = NPIX // BAND
GROUPS = HALF // 2
T_PIECES = 2
I_PIECES = 2
LOADS = 6 + 3 * BANDS


def dft_table():
    index = np.arange(NPIX)
    angle = (index[:, None] * index[None, :] % NPIX) * (2.0 * math.pi / NPIX)
    table = np.concatenate([np.cos(angle), np.sin(angle)], 0) / math.sqrt(NPIX)
    return table.astype(np.float32)


def dot_nt(lhs, rhs):
    return lax.dot_general(lhs, rhs, (((1,), (1,)), ((), ())), preferred_element_type=F32)


def dot_nn(lhs, rhs):
    return jnp.dot(lhs, rhs, preferred_element_type=F32)


def half_angle(field):
    y = field * 0.25
    z = y * y
    sine = y * (1.0 + z * (-1.0 / 6 + z * (1.0 / 120 + z * (-1.0 / 5040 + z * (1.0 / 362880)))))
    cosine = 1.0 + z * (-0.5 + z * (1.0 / 24 + z * (-1.0 / 720 + z * (1.0 / 40320 - z * (1.0 / 3628800)))))
    return 1.0 - 2.0 * sine * sine, 2.0 * sine * cosine


def hat(steps, segment):
    return jnp.maximum(0.0, 1.0 - jnp.abs(steps - float(segment * SUBSTEPS)) * (1.0 / SUBSTEPS))


def kernel(
    image_hbm,
    maps_hbm,
    field_hbm,
    rows_hbm,
    cols_hbm,
    measured_hbm,
    time_hbm,
    count_hbm,
    table_hbm,
    gradient_ref,
    residual_ref,
    image,
    maps,
    field,
    rows,
    cols,
    measured,
    table,
    time_ref,
    count_ref,
    base_re,
    base_im,
    cosines,
    sines,
    mix_b,
    mix_a,
    mix_at,
    grid_a,
    grid_b,
    quarters,
    weight_p,
    weight_m,
    samples,
    own_coil,
    own_cos_a,
    own_cos_b,
    own_sin_a,
    own_sin_b,
    own_twice,
    turned,
    image_sum,
    outbox,
    inbox,
    load_sem,
    send_sem,
    recv_sem,
):
    seg = lax.axis_index("seg")
    coil = lax.axis_index("coil")
    block = lax.rem(seg, HALF)
    component = lax.div(seg, HALF)

    barrier = pltpu.get_barrier_semaphore()

    def greet(step, carry):
        pl.semaphore_signal(
            barrier, inc=1, device_id={"coil": lax.rem(coil + step, COILS)}, device_id_type=MESH
        )
        return carry

    def bands(source, target):
        return [(source.at[pl.ds(BAND * n, BAND)], target.at[pl.ds(BAND * n, BAND)]) for n in range(BANDS)]

    banded = list(
        zip(bands(field_hbm, field), bands(image_hbm.at[0], image), bands(maps_hbm.at[0], maps))
    )
    stages = [
        [(table_hbm, table), (cols_hbm.at[0], cols), *banded[0]],
        [(rows_hbm.at[0], rows), (time_hbm, time_ref)],
        *banded[1:],
        [(measured_hbm.at[0, 0], measured), (count_hbm, count_ref)],
    ]
    loads = []
    places = iter(range(LOADS))
    for stage in stages:
        loads.append([])
        for source, target in stage:
            copy = pltpu.make_async_copy(source, target, load_sem.at[next(places)])
            copy.start()
            loads[-1].append(copy)
    lax.fori_loop(1, COILS, greet, 0)

    def arrived(stage):
        for copy in loads[stage]:
            copy.wait()

    arrived(0)

    col_mix = dot_nt(table[...], cols[...])
    cos_mix = col_mix[:NPIX].astype(BF16)
    sin_mix = col_mix[NPIX:].astype(BF16)
    mix_b[:NPIX, :SCOLS] = cos_mix
    mix_b[:NPIX, SCOLS:] = -sin_mix
    mix_b[NPIX : 2 * NPIX, :SCOLS] = sin_mix
    mix_b[NPIX : 2 * NPIX, SCOLS:] = cos_mix
    mix_b[2 * NPIX :, :] = jnp.zeros((16, 2 * SCOLS), BF16)
    def prepare_rows():
        real = dot_nn(rows[...], table[:NPIX]).astype(BF16)
        negative = dot_nn(rows[...], table[NPIX:]).astype(BF16)
        mix_a[:SROWS] = real
        mix_a[SROWS : 2 * SROWS] = -negative
        mix_a[2 * SROWS : 3 * SROWS] = negative
        mix_a[3 * SROWS :] = real

        steps = jnp.transpose(jnp.broadcast_to(time_ref[...].astype(F32), (SCOLS, SROWS)))
        for pair in range(HALF):
            upper = hat(steps, HALF + pair)
            lower = hat(steps, HALF - 1 - pair)
            weight_p[pair] = upper + lower
            weight_m[pair] = upper - lower

    width = OWN_COLS

    near = lax.div(block * width, 128)
    near_lane = pl.multiple_of(near * 128, 128)
    far_lane = pl.multiple_of(jnp.minimum(near + 1, NPIX // 128 - 1) * 128, 128)
    offset = block * width - near_lane
    back_turn = lax.rem(128 - offset, 128)
    strip_lane = lax.broadcasted_iota(jnp.int32, (STRIP, 128), 1)
    unbroken = strip_lane < 128 - offset
    low_lanes = strip_lane < 64

    def prepare_own(start):
        at = slice(start, start + STRIP)

        def own_columns(ref, first):
            near_half = ref[at, pl.ds(pl.multiple_of(first + near_lane, 128), 128)].astype(F32)
            far_half = ref[at, pl.ds(pl.multiple_of(first + far_lane, 128), 128)].astype(F32)
            return jnp.where(
                unbroken, pltpu.roll(near_half, back_turn, 1), pltpu.roll(far_half, back_turn, 1)
            )

        def doubled(low, high):
            return jnp.where(low_lanes, low, pltpu.roll(high, 64, 1))

        own_field = own_columns(field, 0)
        cosine, sine = half_angle(doubled(own_field, own_field))
        own_cos_a[at] = cosine
        own_cos_b[at] = cosine
        own_sin_a[at] = sine
        own_sin_b[at] = -sine
        own_twice[at] = 4.0 * cosine * cosine - 2.0
        map_re, map_im = own_columns(maps, 0), own_columns(maps, NPIX)
        first = jnp.where(component == 0, map_re, -map_im)
        second = jnp.where(component == 0, map_im, map_re)
        own_coil[at] = doubled(first, second)

    def transpose_mix():
        row_mix = dot_nt(table[...], rows[...])
        mix_at[:, :SROWS] = row_mix[:NPIX].astype(BF16)
        mix_at[:, SROWS:] = (-row_mix[NPIX:]).astype(BF16)

    def prepare_strip(start):
        at = slice(start, start + STRIP)
        cosine, sine = half_angle(field[at])
        last_cosine, last_sine = cosine, -sine
        double = 4.0 * cosine * cosine - 2.0
        for pair in range(HALF):
            cosines[pair, at] = cosine.astype(BF16)
            sines[pair, at] = sine.astype(BF16)
            if pair < HALF - 1:
                cosine, last_cosine = double * cosine - last_cosine, cosine
                sine, last_sine = double * sine - last_sine, sine
        im_re = image[at, :NPIX].astype(F32)
        im_im = image[at, NPIX:].astype(F32)
        co_re = maps[at, :NPIX].astype(F32)
        co_im = maps[at, NPIX:].astype(F32)
        base_re[at] = (im_re * co_re - im_im * co_im).astype(BF16)
        base_im[at] = (im_re * co_im + im_im * co_re).astype(BF16)

    def transform(grid, band, group, piece, pieces):
        at = slice(BAND * band, BAND * (band + 1))
        re, im = base_re[at], base_im[at]
        parts = []
        each = 2 // pieces
        for pair in range(2 * group + each * piece, 2 * group + each * (piece + 1)):
            cosine, sine = cosines[pair, at], sines[pair, at]
            parts.append(jnp.concatenate([re * cosine, im * cosine], 1))
            parts.append(jnp.concatenate([re * sine, im * sine], 1))
        rows_each = 4 * BAND // pieces
        grid[piece * rows_each : (piece + 1) * rows_each] = dot_nn(
            jnp.concatenate(parts, 0), mix_b[: 2 * NPIX]
        ).astype(BF16)

    def add_samples(grid, band, group, piece, pieces):
        rows_each = 2 * SROWS // pieces
        at = slice(piece * rows_each, (piece + 1) * rows_each)
        start = piece * rows_each % SROWS
        band_at = slice(BAND * band, BAND * (band + 1))
        turned_at = slice(2 * SROWS + at.start, 2 * SROWS + at.stop)
        scales = []
        for pair in range(2):
            for weight, rows_at in ((weight_p, at), (weight_m, turned_at)):
                short = weight[2 * group + pair, start : start + rows_each].astype(BF16)
                scales.append(short * mix_a[rows_at, band_at])
        found = dot_nn(jnp.concatenate(scales, 1), grid[...])
        quarters[at] = found if band == group == 0 else quarters[at] + found

    for start in range(0, BAND, STRIP):
        prepare_strip(start)
    order = [(band, group) for band in range(BANDS) for group in range(GROUPS)]
    both_grids = (grid_a, grid_b)
    for step in range(len(order) + 1):
        jobs = []
        if step < len(order):
            band, group = order[step]
            if band + 1 < BANDS:
                if group == 0:
                    arrived(2 + band)
                each = BAND // GROUPS
                first = BAND * (band + 1) + each * group
                jobs = [functools.partial(prepare_strip, start) for start in range(first, first + each, STRIP)]
            else:
                each = NPIX // GROUPS
                first = each * group
                jobs = [functools.partial(prepare_own, start) for start in range(first, first + each, STRIP)]
        if step == 1:
            arrived(1)
            prepare_rows()
        work = []
        if step < len(order):
            work += [
                functools.partial(transform, both_grids[step % 2], *order[step], piece, T_PIECES)
                for piece in range(T_PIECES)
            ]
        if step > 0:
            work += [
                functools.partial(add_samples, both_grids[(step - 1) % 2], *order[step - 1], piece, I_PIECES)
                for piece in range(I_PIECES)
            ]
        if step == 2:
            work.append(transpose_mix)
        for slot, task in enumerate(work):
            for job in jobs[len(jobs) * slot // len(work) : len(jobs) * (slot + 1) // len(work)]:
                job()
            task()

    top, bottom = quarters[:SROWS], quarters[SROWS:]
    samples[:, :SCOLS] = top[:, :SCOLS] - bottom[:, SCOLS:]
    samples[:, SCOLS:] = top[:, SCOLS:] + bottom[:, :SCOLS]

    arrived(1 + BANDS)
    row_ids = lax.broadcasted_iota(jnp.int32, (SROWS, 2 * SCOLS), 0)
    misfit = jnp.where(row_ids < count_ref[0], samples[...] - measured[...].astype(F32), 0.0)
    samples[...] = misfit
    share = SROWS // NSEG
    residual_ref[...] = samples[pl.ds(pl.multiple_of(seg * share, share), share)]

    first = pl.multiple_of(block * width, 16)
    own_mix = jnp.concatenate([mix_b[pl.ds(first, 64)], mix_b[pl.ds(first + NPIX, 64)]], 0)
    turn = dot_nt(misfit.astype(BF16), own_mix)
    lane = lax.broadcasted_iota(jnp.int32, (SROWS, 128), 1)
    swapped = pltpu.roll(turn, 64, 1)
    turned[0] = turn
    turned[1] = jnp.where(lane < 64, swapped, -swapped)
    image_sum[...] = jnp.zeros((NPIX, 128), F32)

    def add_image(pair, now_cos, other_cos, now_sin, other_sin):
        plus = weight_p[pair]
        minus = weight_m[pair]
        top = jnp.concatenate([plus * turned[0], minus * turned[1]], 1)
        bottom = jnp.concatenate([plus * turned[1], -minus * turned[0]], 1)
        spread = jnp.concatenate([top, bottom], 0).astype(BF16)
        back = dot_nn(mix_at[...], spread)
        cosine = now_cos[...]
        sine = now_sin[...]
        image_sum[...] += cosine * back[:, :128] + sine * back[:, 128:]
        other_cos[...] = own_twice[...] * cosine - other_cos[...]
        other_sin[...] = own_twice[...] * sine - other_sin[...]

    for pair in range(HALF):
        if pair % 2 == 0:
            add_image(pair, own_cos_a, own_cos_b, own_sin_a, own_sin_b)
        else:
            add_image(pair, own_cos_b, own_cos_a, own_sin_b, own_sin_a)

    value = image_sum[...] * own_coil[...]
    image_sum[...] = value + pltpu.roll(value, 64, 1)
    half = OWN_ROWS // 2
    tile_lane = lax.broadcasted_iota(jnp.int32, (half, 128), 1)
    for target in range(COILS):
        first_row = target * OWN_ROWS
        outbox[target] = jnp.where(
            tile_lane < 64,
            image_sum[first_row : first_row + half],
            image_sum[first_row + half : first_row + OWN_ROWS],
        )

    pl.semaphore_wait(barrier, COILS - 1)

    def send(step, carry):
        target = lax.rem(coil + step, COILS)
        pltpu.make_async_remote_copy(
            src_ref=outbox.at[target],
            dst_ref=inbox.at[step - 1],
            send_sem=send_sem,
            recv_sem=recv_sem,
            device_id={"coil": target},
            device_id_type=MESH,
        ).start()
        return carry

    lax.fori_loop(1, COILS, send, 0)
    everything = pltpu.make_async_remote_copy(
        src_ref=outbox.at[pl.ds(0, COILS - 1)],
        dst_ref=inbox,
        send_sem=send_sem,
        recv_sem=recv_sem,
        device_id={"coil": lax.rem(coil + 1, COILS)},
        device_id_type=MESH,
    )
    everything.wait_recv()
    total = outbox[coil]
    for slot in range(COILS - 1):
        total = total + inbox[slot]
    total = total * (COILS ** -0.5)
    gradient_ref[:half] = total
    gradient_ref[half:] = total[:2]
    everything.wait_send()


def finish(total_ref, misfit_ref, gradient_ref, residual_ref):
    half = OWN_ROWS // 2
    total = total_ref[:half]
    gradient_ref[:half, 0] = total[:, :OWN_COLS]
    gradient_ref[half:, 0] = pltpu.roll(total, 64, 1)[:, :OWN_COLS]
    residual_ref[0, 0] = misfit_ref[...]


def shards(*arguments):
    vmem = pl.BlockSpec(memory_space=pltpu.VMEM)
    anywhere = pl.BlockSpec(memory_space=pl.ANY)
    square = pltpu.VMEM((NPIX, NPIX), F32)
    own = pltpu.VMEM((NPIX, 128), F32)
    total, misfit = (
        pl.pallas_call(
            kernel,
            out_shape=(
                jax.ShapeDtypeStruct((8, 128), F32),
                jax.ShapeDtypeStruct((SROWS // NSEG, 2 * SCOLS), F32),
            ),
            in_specs=[anywhere] * 9,
            out_specs=(vmem, vmem),
            scratch_shapes=[
                pltpu.VMEM((NPIX, 2 * NPIX), BF16),
                pltpu.VMEM((NPIX, 2 * NPIX), BF16),
                square,
                pltpu.VMEM((SROWS, NPIX), BF16),
                pltpu.VMEM((SCOLS, NPIX), BF16),
                pltpu.VMEM((SROWS, 2 * SCOLS), BF16),
                pltpu.VMEM((2 * NPIX, NPIX), BF16),
                pltpu.VMEM((1, SROWS), jnp.int32),
                pltpu.SMEM((1,), jnp.int32),
                pltpu.VMEM((NPIX, NPIX), BF16),
                pltpu.VMEM((NPIX, NPIX), BF16),
                pltpu.VMEM((HALF, NPIX, NPIX), BF16),
                pltpu.VMEM((HALF, NPIX, NPIX), BF16),
                pltpu.VMEM((2 * NPIX + 16, 2 * SCOLS), BF16),
                pltpu.VMEM((4 * SROWS, NPIX), BF16),
                pltpu.VMEM((NPIX, 2 * SROWS), BF16),
                pltpu.VMEM((4 * BAND, 2 * SCOLS), BF16),
                pltpu.VMEM((4 * BAND, 2 * SCOLS), BF16),
                pltpu.VMEM((2 * SROWS, 2 * SCOLS), F32),
                pltpu.VMEM((HALF, SROWS, SCOLS), F32),
                pltpu.VMEM((HALF, SROWS, SCOLS), F32),
                pltpu.VMEM((SROWS, 2 * SCOLS), F32),
                own,
                own,
                own,
                own,
                own,
                own,
                pltpu.VMEM((2, SROWS, 128), F32),
                own,
                pltpu.VMEM((COILS, OWN_ROWS // 2, 128), F32),
                pltpu.VMEM((COILS - 1, OWN_ROWS // 2, 128), F32),
                pltpu.SemaphoreType.DMA((LOADS,)),
                pltpu.SemaphoreType.DMA,
                pltpu.SemaphoreType.DMA,
            ],
            compiler_params=pltpu.CompilerParams(
                collective_id=0, has_side_effects=True, vmem_limit_bytes=60 * 2**20
            ),
        )(*arguments, jnp.asarray(dft_table()).astype(BF16))
    )

    gradient, residual = pl.pallas_call(
        finish,
        out_shape=(
            jax.ShapeDtypeStruct((OWN_ROWS, 1, OWN_COLS), F32),
            jax.ShapeDtypeStruct((1, 1, SROWS // NSEG, 2 * SCOLS), F32),
        ),
        in_specs=[vmem, vmem],
        out_specs=(vmem, vmem),
    )(total, misfit)
    return jnp.transpose(gradient, (1, 0, 2)), residual


def solution(mesh):
    in_specs = (P(), P("coil", None, None), P(), P(), P(), P("coil", None, None, None), P(), P())
    out_specs = (P(None, "coil", "seg"), P("coil", None, "seg", None))
    return jax.shard_map(shards, mesh=mesh, in_specs=in_specs, out_specs=out_specs, check_vma=False)
```

```python
import functools
import math

import jax
import jax.numpy as jnp
import numpy as np
from jax import lax
from jax.experimental import pallas as pl
from jax.experimental.pallas import tpu as pltpu
from jax.sharding import PartitionSpec as P

SUBSTEPS = 4
NPIX = 384
SROWS = 256
SCOLS = 128
NSEG = 16
HALF = NSEG // 2
COILS = 32
OWN_ROWS = NPIX // COILS
OWN_COLS = 2 * NPIX // NSEG
MESH = pl.DeviceIdType.MESH
F32 = jnp.float32
BF16 = jnp.bfloat16
STRIP = 16
BAND = 128
BANDS = NPIX // BAND
GROUPS = HALF // 2
T_PIECES = 2
I_PIECES = 2
LOADS = 6 + 3 * BANDS


def dft_table():
    index = np.arange(NPIX)
    angle = (index[:, None] * index[None, :] % NPIX) * (2.0 * math.pi / NPIX)
    table = np.concatenate([np.cos(angle), np.sin(angle)], 0) / math.sqrt(NPIX)
    return table.astype(np.float32)


def dot_nt(lhs, rhs):
    return lax.dot_general(lhs, rhs, (((1,), (1,)), ((), ())), preferred_element_type=F32)


def dot_nn(lhs, rhs):
    return jnp.dot(lhs, rhs, preferred_element_type=F32)


def half_angle(field):
    y = field * 0.25
    z = y * y
    sine = y * (1.0 + z * (-1.0 / 6 + z * (1.0 / 120 + z * (-1.0 / 5040 + z * (1.0 / 362880)))))
    cosine = 1.0 + z * (-0.5 + z * (1.0 / 24 + z * (-1.0 / 720 + z * (1.0 / 40320 - z * (1.0 / 3628800)))))
    return 1.0 - 2.0 * sine * sine, 2.0 * sine * cosine


def hat(steps, segment):
    return jnp.maximum(0.0, 1.0 - jnp.abs(steps - float(segment * SUBSTEPS)) * (1.0 / SUBSTEPS))


def kernel(
    image_hbm,
    maps_hbm,
    field_hbm,
    rows_hbm,
    cols_hbm,
    measured_hbm,
    time_hbm,
    count_hbm,
    table_hbm,
    gradient_ref,
    residual_ref,
    image,
    maps,
    field,
    rows,
    cols,
    measured,
    table,
    time_ref,
    count_ref,
    base_re,
    base_im,
    cosines,
    sines,
    mix_b,
    mix_a,
    mix_at,
    grid_a,
    grid_b,
    quarters,
    weight_p,
    weight_m,
    samples,
    own_coil,
    own_cos_a,
    own_cos_b,
    own_sin_a,
    own_sin_b,
    own_twice,
    turned,
    image_sum,
    outbox,
    inbox,
    load_sem,
    send_sem,
    recv_sem,
):
    seg = lax.axis_index("seg")
    coil = lax.axis_index("coil")
    block = lax.rem(seg, HALF)
    component = lax.div(seg, HALF)

    barrier = pltpu.get_barrier_semaphore()

    def greet(step, carry):
        pl.semaphore_signal(
            barrier, inc=1, device_id={"coil": lax.rem(coil + step, COILS)}, device_id_type=MESH
        )
        return carry

    def bands(source, target):
        return [(source.at[pl.ds(BAND * n, BAND)], target.at[pl.ds(BAND * n, BAND)]) for n in range(BANDS)]

    banded = list(
        zip(bands(field_hbm, field), bands(image_hbm.at[0], image), bands(maps_hbm.at[0], maps))
    )
    stages = [
        [(table_hbm, table), (cols_hbm.at[0], cols), *banded[0]],
        [(rows_hbm.at[0], rows), (time_hbm, time_ref)],
        *banded[1:],
        [(measured_hbm.at[0, 0], measured), (count_hbm, count_ref)],
    ]
    loads = []
    places = iter(range(LOADS))
    for stage in stages:
        loads.append([])
        for source, target in stage:
            copy = pltpu.make_async_copy(source, target, load_sem.at[next(places)])
            copy.start()
            loads[-1].append(copy)
    lax.fori_loop(1, COILS, greet, 0)

    def arrived(stage):
        for copy in loads[stage]:
            copy.wait()

    arrived(0)

    col_mix = dot_nt(table[...], cols[...])
    cos_mix = col_mix[:NPIX].astype(BF16)
    sin_mix = col_mix[NPIX:].astype(BF16)
    mix_b[:NPIX, :SCOLS] = cos_mix
    mix_b[:NPIX, SCOLS:] = -sin_mix
    mix_b[NPIX : 2 * NPIX, :SCOLS] = sin_mix
    mix_b[NPIX : 2 * NPIX, SCOLS:] = cos_mix
    mix_b[2 * NPIX :, :] = jnp.zeros((16, 2 * SCOLS), BF16)
    def prepare_rows():
        real = dot_nn(rows[...], table[:NPIX]).astype(BF16)
        negative = dot_nn(rows[...], table[NPIX:]).astype(BF16)
        mix_a[:SROWS] = real
        mix_a[SROWS : 2 * SROWS] = -negative
        mix_a[2 * SROWS : 3 * SROWS] = negative
        mix_a[3 * SROWS :] = real

        steps = jnp.transpose(jnp.broadcast_to(time_ref[...].astype(F32), (SCOLS, SROWS)))
        for pair in range(HALF):
            upper = hat(steps, HALF + pair)
            lower = hat(steps, HALF - 1 - pair)
            weight_p[pair] = upper + lower
            weight_m[pair] = upper - lower

    width = OWN_COLS

    near = lax.div(block * width, 128)
    near_lane = pl.multiple_of(near * 128, 128)
    far_lane = pl.multiple_of(jnp.minimum(near + 1, NPIX // 128 - 1) * 128, 128)
    offset = block * width - near_lane
    back_turn = lax.rem(128 - offset, 128)
    strip_lane = lax.broadcasted_iota(jnp.int32, (STRIP, 128), 1)
    unbroken = strip_lane < 128 - offset
    low_lanes = strip_lane < 64

    def prepare_own(start):
        at = slice(start, start + STRIP)

        def own_columns(ref, first):
            near_half = ref[at, pl.ds(pl.multiple_of(first + near_lane, 128), 128)].astype(F32)
            far_half = ref[at, pl.ds(pl.multiple_of(first + far_lane, 128), 128)].astype(F32)
            return jnp.where(
                unbroken, pltpu.roll(near_half, back_turn, 1), pltpu.roll(far_half, back_turn, 1)
            )

        def doubled(low, high):
            return jnp.where(low_lanes, low, pltpu.roll(high, 64, 1))

        own_field = own_columns(field, 0)
        cosine, sine = half_angle(doubled(own_field, own_field))
        own_cos_a[at] = cosine
        own_cos_b[at] = cosine
        own_sin_a[at] = sine
        own_sin_b[at] = -sine
        own_twice[at] = 4.0 * cosine * cosine - 2.0
        map_re, map_im = own_columns(maps, 0), own_columns(maps, NPIX)
        first = jnp.where(component == 0, map_re, -map_im)
        second = jnp.where(component == 0, map_im, map_re)
        own_coil[at] = doubled(first, second)

    def transpose_mix():
        row_mix = dot_nt(table[...], rows[...])
        mix_at[:, :SROWS] = row_mix[:NPIX].astype(BF16)
        mix_at[:, SROWS:] = (-row_mix[NPIX:]).astype(BF16)

    def prepare_strip(start):
        at = slice(start, start + STRIP)
        cosine, sine = half_angle(field[at])
        last_cosine, last_sine = cosine, -sine
        double = 4.0 * cosine * cosine - 2.0
        for pair in range(HALF):
            cosines[pair, at] = cosine.astype(BF16)
            sines[pair, at] = sine.astype(BF16)
            if pair < HALF - 1:
                cosine, last_cosine = double * cosine - last_cosine, cosine
                sine, last_sine = double * sine - last_sine, sine
        im_re = image[at, :NPIX].astype(F32)
        im_im = image[at, NPIX:].astype(F32)
        co_re = maps[at, :NPIX].astype(F32)
        co_im = maps[at, NPIX:].astype(F32)
        base_re[at] = (im_re * co_re - im_im * co_im).astype(BF16)
        base_im[at] = (im_re * co_im + im_im * co_re).astype(BF16)

    def transform(grid, band, group, piece, pieces):
        at = slice(BAND * band, BAND * (band + 1))
        re, im = base_re[at], base_im[at]
        parts = []
        each = 2 // pieces
        for pair in range(2 * group + each * piece, 2 * group + each * (piece + 1)):
            cosine, sine = cosines[pair, at], sines[pair, at]
            parts.append(jnp.concatenate([re * cosine, im * cosine], 1))
            parts.append(jnp.concatenate([re * sine, im * sine], 1))
        rows_each = 4 * BAND // pieces
        grid[piece * rows_each : (piece + 1) * rows_each] = dot_nn(
            jnp.concatenate(parts, 0), mix_b[: 2 * NPIX]
        ).astype(BF16)

    def add_samples(grid, band, group, piece, pieces):
        rows_each = 2 * SROWS // pieces
        at = slice(piece * rows_each, (piece + 1) * rows_each)
        start = piece * rows_each % SROWS
        band_at = slice(BAND * band, BAND * (band + 1))
        turned_at = slice(2 * SROWS + at.start, 2 * SROWS + at.stop)
        scales = []
        for pair in range(2):
            for weight, rows_at in ((weight_p, at), (weight_m, turned_at)):
                short = weight[2 * group + pair, start : start + rows_each].astype(BF16)
                scales.append(short * mix_a[rows_at, band_at])
        found = dot_nn(jnp.concatenate(scales, 1), grid[...])
        quarters[at] = found if band == group == 0 else quarters[at] + found

    for start in range(0, BAND, STRIP):
        prepare_strip(start)
    order = [(band, group) for band in range(BANDS) for group in range(GROUPS)]
    both_grids = (grid_a, grid_b)
    for step in range(len(order) + 1):
        jobs = []
        if step < len(order):
            band, group = order[step]
            if band + 1 < BANDS:
                if group == 0:
                    arrived(2 + band)
                each = BAND // GROUPS
                first = BAND * (band + 1) + each * group
                jobs = [functools.partial(prepare_strip, start) for start in range(first, first + each, STRIP)]
            else:
                each = NPIX // GROUPS
                first = each * group
                jobs = [functools.partial(prepare_own, start) for start in range(first, first + each, STRIP)]
        if step == 1:
            arrived(1)
            prepare_rows()
        work = []
        if step < len(order):
            work += [
                functools.partial(transform, both_grids[step % 2], *order[step], piece, T_PIECES)
                for piece in range(T_PIECES)
            ]
        if step > 0:
            work += [
                functools.partial(add_samples, both_grids[(step - 1) % 2], *order[step - 1], piece, I_PIECES)
                for piece in range(I_PIECES)
            ]
        if step == 2:
            work.append(transpose_mix)
        for slot, task in enumerate(work):
            for job in jobs[len(jobs) * slot // len(work) : len(jobs) * (slot + 1) // len(work)]:
                job()
            task()

    top, bottom = quarters[:SROWS], quarters[SROWS:]
    samples[:, :SCOLS] = top[:, :SCOLS] - bottom[:, SCOLS:]
    samples[:, SCOLS:] = top[:, SCOLS:] + bottom[:, :SCOLS]

    arrived(1 + BANDS)
    row_ids = lax.broadcasted_iota(jnp.int32, (SROWS, 2 * SCOLS), 0)
    misfit = jnp.where(row_ids < count_ref[0], samples[...] - measured[...].astype(F32), 0.0)
    samples[...] = misfit
    share = SROWS // NSEG
    residual_ref[...] = samples[pl.ds(pl.multiple_of(seg * share, share), share)]

    first = pl.multiple_of(block * width, 16)
    own_mix = jnp.concatenate([mix_b[pl.ds(first, 64)], mix_b[pl.ds(first + NPIX, 64)]], 0)
    turn = dot_nt(misfit.astype(BF16), own_mix)
    lane = lax.broadcasted_iota(jnp.int32, (SROWS, 128), 1)
    swapped = pltpu.roll(turn, 64, 1)
    turned[0] = turn
    turned[1] = jnp.where(lane < 64, swapped, -swapped)
    image_sum[...] = jnp.zeros((NPIX, 128), F32)

    def add_image(pair, now_cos, other_cos, now_sin, other_sin):
        plus = weight_p[pair]
        minus = weight_m[pair]
        top = jnp.concatenate([plus * turned[0], minus * turned[1]], 1)
        bottom = jnp.concatenate([plus * turned[1], -minus * turned[0]], 1)
        spread = jnp.concatenate([top, bottom], 0).astype(BF16)
        back = dot_nn(mix_at[...], spread)
        cosine = now_cos[...]
        sine = now_sin[...]
        image_sum[...] += cosine * back[:, :128] + sine * back[:, 128:]
        other_cos[...] = own_twice[...] * cosine - other_cos[...]
        other_sin[...] = own_twice[...] * sine - other_sin[...]

    for pair in range(HALF):
        if pair % 2 == 0:
            add_image(pair, own_cos_a, own_cos_b, own_sin_a, own_sin_b)
        else:
            add_image(pair, own_cos_b, own_cos_a, own_sin_b, own_sin_a)

    value = image_sum[...] * own_coil[...]
    image_sum[...] = value + pltpu.roll(value, 64, 1)
    half = OWN_ROWS // 2
    tile_lane = lax.broadcasted_iota(jnp.int32, (half, 128), 1)
    for target in range(COILS):
        first_row = target * OWN_ROWS
        outbox[target] = jnp.where(
            tile_lane < 64,
            image_sum[first_row : first_row + half],
            image_sum[first_row + half : first_row + OWN_ROWS],
        )

    pl.semaphore_wait(barrier, COILS - 1)

    def send(step, carry):
        target = lax.rem(coil + step, COILS)
        pltpu.make_async_remote_copy(
            src_ref=outbox.at[target],
            dst_ref=inbox.at[step - 1],
            send_sem=send_sem,
            recv_sem=recv_sem,
            device_id={"coil": target},
            device_id_type=MESH,
        ).start()
        return carry

    lax.fori_loop(1, COILS, send, 0)
    everything = pltpu.make_async_remote_copy(
        src_ref=outbox.at[pl.ds(0, COILS - 1)],
        dst_ref=inbox,
        send_sem=send_sem,
        recv_sem=recv_sem,
        device_id={"coil": lax.rem(coil + 1, COILS)},
        device_id_type=MESH,
    )
    everything.wait_recv()
    total = outbox[coil]
    for slot in range(COILS - 1):
        total = total + inbox[slot]
    total = total * (COILS ** -0.5)
    gradient_ref[:half] = total
    gradient_ref[half:] = total[:2]
    everything.wait_send()


def finish(total_ref, misfit_ref, gradient_ref, residual_ref):
    half = OWN_ROWS // 2
    total = total_ref[:half]
    gradient_ref[:half, 0] = total[:, :OWN_COLS]
    gradient_ref[half:, 0] = pltpu.roll(total, 64, 1)[:, :OWN_COLS]
    residual_ref[0, 0] = misfit_ref[...]


def shards(*arguments):
    vmem = pl.BlockSpec(memory_space=pltpu.VMEM)
    anywhere = pl.BlockSpec(memory_space=pl.ANY)
    square = pltpu.VMEM((NPIX, NPIX), F32)
    own = pltpu.VMEM((NPIX, 128), F32)
    total, misfit = (
        pl.pallas_call(
            kernel,
            out_shape=(
                jax.ShapeDtypeStruct((8, 128), F32),
                jax.ShapeDtypeStruct((SROWS // NSEG, 2 * SCOLS), F32),
            ),
            in_specs=[anywhere] * 9,
            out_specs=(vmem, vmem),
            scratch_shapes=[
                pltpu.VMEM((NPIX, 2 * NPIX), BF16),
                pltpu.VMEM((NPIX, 2 * NPIX), BF16),
                square,
                pltpu.VMEM((SROWS, NPIX), BF16),
                pltpu.VMEM((SCOLS, NPIX), BF16),
                pltpu.VMEM((SROWS, 2 * SCOLS), BF16),
                pltpu.VMEM((2 * NPIX, NPIX), BF16),
                pltpu.VMEM((1, SROWS), jnp.int32),
                pltpu.SMEM((1,), jnp.int32),
                pltpu.VMEM((NPIX, NPIX), BF16),
                pltpu.VMEM((NPIX, NPIX), BF16),
                pltpu.VMEM((HALF, NPIX, NPIX), BF16),
                pltpu.VMEM((HALF, NPIX, NPIX), BF16),
                pltpu.VMEM((2 * NPIX + 16, 2 * SCOLS), BF16),
                pltpu.VMEM((4 * SROWS, NPIX), BF16),
                pltpu.VMEM((NPIX, 2 * SROWS), BF16),
                pltpu.VMEM((4 * BAND, 2 * SCOLS), BF16),
                pltpu.VMEM((4 * BAND, 2 * SCOLS), BF16),
                pltpu.VMEM((2 * SROWS, 2 * SCOLS), F32),
                pltpu.VMEM((HALF, SROWS, SCOLS), F32),
                pltpu.VMEM((HALF, SROWS, SCOLS), F32),
                pltpu.VMEM((SROWS, 2 * SCOLS), F32),
                own,
                own,
                own,
                own,
                own,
                own,
                pltpu.VMEM((2, SROWS, 128), F32),
                own,
                pltpu.VMEM((COILS, OWN_ROWS // 2, 128), F32),
                pltpu.VMEM((COILS - 1, OWN_ROWS // 2, 128), F32),
                pltpu.SemaphoreType.DMA((LOADS,)),
                pltpu.SemaphoreType.DMA,
                pltpu.SemaphoreType.DMA,
            ],
            compiler_params=pltpu.CompilerParams(
                collective_id=0, has_side_effects=True, vmem_limit_bytes=55160 * 2**10
            ),
        )(*arguments, jnp.asarray(dft_table()).astype(BF16))
    )

    gradient, residual = pl.pallas_call(
        finish,
        out_shape=(
            jax.ShapeDtypeStruct((OWN_ROWS, 1, OWN_COLS), F32),
            jax.ShapeDtypeStruct((1, 1, SROWS // NSEG, 2 * SCOLS), F32),
        ),
        in_specs=[vmem, vmem],
        out_specs=(vmem, vmem),
        compiler_params=pltpu.CompilerParams(vmem_limit_bytes=1 * 2**20),
    )(total, misfit)
    return jnp.transpose(gradient, (1, 0, 2)), residual


def solution(mesh):
    in_specs = (P(), P("coil", None, None), P(), P(), P(), P("coil", None, None, None), P(), P())
    out_specs = (P(None, "coil", "seg"), P("coil", None, "seg", None))
    return jax.shard_map(shards, mesh=mesh, in_specs=in_specs, out_specs=out_specs, check_vma=False)
```

```python
import functools
import math

import jax
import jax.numpy as jnp
import numpy as np
from jax import lax
from jax.experimental import pallas as pl
from jax.experimental.pallas import tpu as pltpu
from jax.sharding import PartitionSpec as P

SUBSTEPS = 4
NPIX = 384
SROWS = 256
SCOLS = 128
NSEG = 16
HALF = NSEG // 2
COILS = 32
OWN_ROWS = NPIX // COILS
OWN_COLS = 2 * NPIX // NSEG
MESH = pl.DeviceIdType.MESH
F32 = jnp.float32
BF16 = jnp.bfloat16
STRIP = 16
BAND = 128
BANDS = NPIX // BAND
GROUPS = HALF // 2
T_PIECES = 2
I_PIECES = 2
LOADS = 6 + 3 * BANDS


def dft_table():
    index = np.arange(NPIX)
    angle = (index[:, None] * index[None, :] % NPIX) * (2.0 * math.pi / NPIX)
    table = np.concatenate([np.cos(angle), np.sin(angle)], 0) / math.sqrt(NPIX)
    return table.astype(np.float32)


def dot_nt(lhs, rhs):
    return lax.dot_general(lhs, rhs, (((1,), (1,)), ((), ())), preferred_element_type=F32)


def dot_nn(lhs, rhs):
    return jnp.dot(lhs, rhs, preferred_element_type=F32)


def half_angle(field):
    y = field * 0.25
    z = y * y
    sine = y * (1.0 + z * (-1.0 / 6 + z * (1.0 / 120 + z * (-1.0 / 5040 + z * (1.0 / 362880)))))
    cosine = 1.0 + z * (-0.5 + z * (1.0 / 24 + z * (-1.0 / 720 + z * (1.0 / 40320 - z * (1.0 / 3628800)))))
    return 1.0 - 2.0 * sine * sine, 2.0 * sine * cosine


def hat(steps, segment):
    return jnp.maximum(0.0, 1.0 - jnp.abs(steps - float(segment * SUBSTEPS)) * (1.0 / SUBSTEPS))


def kernel(
    image_hbm,
    maps_hbm,
    field_hbm,
    rows_hbm,
    cols_hbm,
    measured_hbm,
    time_hbm,
    count_hbm,
    table_hbm,
    gradient_ref,
    residual_ref,
    image,
    maps,
    field,
    rows,
    cols,
    measured,
    table,
    time_ref,
    count_ref,
    base_re,
    base_im,
    cosines,
    sines,
    mix_b,
    mix_a,
    mix_at,
    grid_a,
    grid_b,
    quarters,
    weight_p,
    weight_m,
    samples,
    own_coil,
    own_cos_a,
    own_cos_b,
    own_sin_a,
    own_sin_b,
    own_twice,
    turned,
    image_sum,
    outbox,
    inbox,
    load_sem,
    send_sem,
    recv_sem,
):
    seg = lax.axis_index("seg")
    coil = lax.axis_index("coil")
    block = lax.rem(seg, HALF)
    component = lax.div(seg, HALF)

    barrier = pltpu.get_barrier_semaphore()

    def greet(step, carry):
        pl.semaphore_signal(
            barrier, inc=1, device_id={"coil": lax.rem(coil + step, COILS)}, device_id_type=MESH
        )
        return carry

    def bands(source, target):
        return [(source.at[pl.ds(BAND * n, BAND)], target.at[pl.ds(BAND * n, BAND)]) for n in range(BANDS)]

    banded = list(
        zip(bands(field_hbm, field), bands(image_hbm.at[0], image), bands(maps_hbm.at[0], maps))
    )
    stages = [
        [(table_hbm, table), (cols_hbm.at[0], cols), *banded[0]],
        [(rows_hbm.at[0], rows), (time_hbm, time_ref)],
        *banded[1:],
        [(measured_hbm.at[0, 0], measured), (count_hbm, count_ref)],
    ]
    loads = []
    places = iter(range(LOADS))
    for stage in stages:
        loads.append([])
        for source, target in stage:
            copy = pltpu.make_async_copy(source, target, load_sem.at[next(places)])
            copy.start()
            loads[-1].append(copy)
    lax.fori_loop(1, COILS, greet, 0)

    def arrived(stage):
        for copy in loads[stage]:
            copy.wait()

    arrived(0)

    col_mix = dot_nt(table[...], cols[...])
    cos_mix = col_mix[:NPIX].astype(BF16)
    sin_mix = col_mix[NPIX:].astype(BF16)
    mix_b[:NPIX, :SCOLS] = cos_mix
    mix_b[:NPIX, SCOLS:] = -sin_mix
    mix_b[NPIX : 2 * NPIX, :SCOLS] = sin_mix
    mix_b[NPIX : 2 * NPIX, SCOLS:] = cos_mix
    mix_b[2 * NPIX :, :] = jnp.zeros((16, 2 * SCOLS), BF16)
    def prepare_rows():
        real = dot_nn(rows[...], table[:NPIX]).astype(BF16)
        negative = dot_nn(rows[...], table[NPIX:]).astype(BF16)
        mix_a[:SROWS] = real
        mix_a[SROWS : 2 * SROWS] = -negative
        mix_a[2 * SROWS : 3 * SROWS] = negative
        mix_a[3 * SROWS :] = real

        steps = jnp.transpose(jnp.broadcast_to(time_ref[...].astype(F32), (SCOLS, SROWS)))
        for pair in range(HALF):
            upper = hat(steps, HALF + pair)
            lower = hat(steps, HALF - 1 - pair)
            weight_p[pair] = upper + lower
            weight_m[pair] = upper - lower

    width = OWN_COLS

    near = lax.div(block * width, 128)
    near_lane = pl.multiple_of(near * 128, 128)
    far_lane = pl.multiple_of(jnp.minimum(near + 1, NPIX // 128 - 1) * 128, 128)
    offset = block * width - near_lane
    back_turn = lax.rem(128 - offset, 128)
    strip_lane = lax.broadcasted_iota(jnp.int32, (STRIP, 128), 1)
    unbroken = strip_lane < 128 - offset
    low_lanes = strip_lane < 64

    def prepare_own(start):
        at = slice(start, start + STRIP)

        def own_columns(ref, first):
            near_half = ref[at, pl.ds(pl.multiple_of(first + near_lane, 128), 128)].astype(F32)
            far_half = ref[at, pl.ds(pl.multiple_of(first + far_lane, 128), 128)].astype(F32)
            return jnp.where(
                unbroken, pltpu.roll(near_half, back_turn, 1), pltpu.roll(far_half, back_turn, 1)
            )

        def doubled(low, high):
            return jnp.where(low_lanes, low, pltpu.roll(high, 64, 1))

        own_field = own_columns(field, 0)
        cosine, sine = half_angle(doubled(own_field, own_field))
        own_cos_a[at] = cosine
        own_cos_b[at] = cosine
        own_sin_a[at] = sine
        own_sin_b[at] = -sine
        own_twice[at] = 4.0 * cosine * cosine - 2.0
        map_re, map_im = own_columns(maps, 0), own_columns(maps, NPIX)
        first = jnp.where(component == 0, map_re, -map_im)
        second = jnp.where(component == 0, map_im, map_re)
        own_coil[at] = doubled(first, second)

    def transpose_mix():
        row_mix = dot_nt(table[...], rows[...])
        mix_at[:, :SROWS] = row_mix[:NPIX].astype(BF16)
        mix_at[:, SROWS:] = (-row_mix[NPIX:]).astype(BF16)

    def prepare_strip(start):
        at = slice(start, start + STRIP)
        cosine, sine = half_angle(field[at])
        last_cosine, last_sine = cosine, -sine
        double = 4.0 * cosine * cosine - 2.0
        for pair in range(HALF):
            cosines[pair, at] = cosine.astype(BF16)
            sines[pair, at] = sine.astype(BF16)
            if pair < HALF - 1:
                cosine, last_cosine = double * cosine - last_cosine, cosine
                sine, last_sine = double * sine - last_sine, sine
        im_re = image[at, :NPIX].astype(F32)
        im_im = image[at, NPIX:].astype(F32)
        co_re = maps[at, :NPIX].astype(F32)
        co_im = maps[at, NPIX:].astype(F32)
        base_re[at] = (im_re * co_re - im_im * co_im).astype(BF16)
        base_im[at] = (im_re * co_im + im_im * co_re).astype(BF16)

    def transform(grid, band, group, piece, pieces):
        at = slice(BAND * band, BAND * (band + 1))
        re, im = base_re[at], base_im[at]
        parts = []
        each = 2 // pieces
        for pair in range(2 * group + each * piece, 2 * group + each * (piece + 1)):
            cosine, sine = cosines[pair, at], sines[pair, at]
            parts.append(jnp.concatenate([re * cosine, im * cosine], 1))
            parts.append(jnp.concatenate([re * sine, im * sine], 1))
        rows_each = 4 * BAND // pieces
        grid[piece * rows_each : (piece + 1) * rows_each] = dot_nn(
            jnp.concatenate(parts, 0), mix_b[: 2 * NPIX]
        ).astype(BF16)

    def add_samples(grid, band, group, piece, pieces):
        rows_each = 2 * SROWS // pieces
        at = slice(piece * rows_each, (piece + 1) * rows_each)
        start = piece * rows_each % SROWS
        band_at = slice(BAND * band, BAND * (band + 1))
        turned_at = slice(2 * SROWS + at.start, 2 * SROWS + at.stop)
        scales = []
        for pair in range(2):
            for weight, rows_at in ((weight_p, at), (weight_m, turned_at)):
                short = weight[2 * group + pair, start : start + rows_each].astype(BF16)
                scales.append(short * mix_a[rows_at, band_at])
        found = dot_nn(jnp.concatenate(scales, 1), grid[...])
        quarters[at] = found if band == group == 0 else quarters[at] + found

    for start in range(0, BAND, STRIP):
        prepare_strip(start)
    order = [(band, group) for band in range(BANDS) for group in range(GROUPS)]
    both_grids = (grid_a, grid_b)
    for step in range(len(order) + 1):
        jobs = []
        if step < len(order):
            band, group = order[step]
            if band + 1 < BANDS:
                if group == 0:
                    arrived(2 + band)
                each = BAND // GROUPS
                first = BAND * (band + 1) + each * group
                jobs = [functools.partial(prepare_strip, start) for start in range(first, first + each, STRIP)]
            else:
                each = NPIX // GROUPS
                first = each * group
                jobs = [functools.partial(prepare_own, start) for start in range(first, first + each, STRIP)]
        if step == 1:
            arrived(1)
            prepare_rows()
        work = []
        if step < len(order):
            work += [
                functools.partial(transform, both_grids[step % 2], *order[step], piece, T_PIECES)
                for piece in range(T_PIECES)
            ]
        if step > 0:
            work += [
                functools.partial(add_samples, both_grids[(step - 1) % 2], *order[step - 1], piece, I_PIECES)
                for piece in range(I_PIECES)
            ]
        if step == 2:
            work.append(transpose_mix)
        for slot, task in enumerate(work):
            for job in jobs[len(jobs) * slot // len(work) : len(jobs) * (slot + 1) // len(work)]:
                job()
            task()

    top, bottom = quarters[:SROWS], quarters[SROWS:]
    samples[:, :SCOLS] = top[:, :SCOLS] - bottom[:, SCOLS:]
    samples[:, SCOLS:] = top[:, SCOLS:] + bottom[:, :SCOLS]

    arrived(1 + BANDS)
    row_ids = lax.broadcasted_iota(jnp.int32, (SROWS, 2 * SCOLS), 0)
    misfit = jnp.where(row_ids < count_ref[0], samples[...] - measured[...].astype(F32), 0.0)
    samples[...] = misfit
    share = SROWS // NSEG
    residual_ref[...] = samples[pl.ds(pl.multiple_of(seg * share, share), share)]

    first = pl.multiple_of(block * width, 16)
    own_mix = jnp.concatenate([mix_b[pl.ds(first, 64)], mix_b[pl.ds(first + NPIX, 64)]], 0)
    turn = dot_nt(misfit.astype(BF16), own_mix)
    lane = lax.broadcasted_iota(jnp.int32, (SROWS, 128), 1)
    swapped = pltpu.roll(turn, 64, 1)
    turned[0] = turn
    turned[1] = jnp.where(lane < 64, swapped, -swapped)
    image_sum[...] = jnp.zeros((NPIX, 128), F32)

    def add_image(pair, now_cos, other_cos, now_sin, other_sin):
        plus = weight_p[pair]
        minus = weight_m[pair]
        top = jnp.concatenate([plus * turned[0], minus * turned[1]], 1)
        bottom = jnp.concatenate([plus * turned[1], -minus * turned[0]], 1)
        spread = jnp.concatenate([top, bottom], 0).astype(BF16)
        back = dot_nn(mix_at[...], spread)
        cosine = now_cos[...]
        sine = now_sin[...]
        image_sum[...] += cosine * back[:, :128] + sine * back[:, 128:]
        other_cos[...] = own_twice[...] * cosine - other_cos[...]
        other_sin[...] = own_twice[...] * sine - other_sin[...]

    for pair in range(HALF):
        if pair % 2 == 0:
            add_image(pair, own_cos_a, own_cos_b, own_sin_a, own_sin_b)
        else:
            add_image(pair, own_cos_b, own_cos_a, own_sin_b, own_sin_a)

    value = image_sum[...] * own_coil[...]
    image_sum[...] = value + pltpu.roll(value, 64, 1)
    half = OWN_ROWS // 2
    tile_lane = lax.broadcasted_iota(jnp.int32, (half, 128), 1)
    for target in range(COILS):
        first_row = target * OWN_ROWS
        outbox[target] = jnp.where(
            tile_lane < 64,
            image_sum[first_row : first_row + half],
            image_sum[first_row + half : first_row + OWN_ROWS],
        )

    pl.semaphore_wait(barrier, COILS - 1)

    def send(step, carry):
        target = lax.rem(coil + step, COILS)
        pltpu.make_async_remote_copy(
            src_ref=outbox.at[target],
            dst_ref=inbox.at[step - 1],
            send_sem=send_sem,
            recv_sem=recv_sem,
            device_id={"coil": target},
            device_id_type=MESH,
        ).start()
        return carry

    for step in range(1, COILS):
        send(step, 0)
    everything = pltpu.make_async_remote_copy(
        src_ref=outbox.at[pl.ds(0, COILS - 1)],
        dst_ref=inbox,
        send_sem=send_sem,
        recv_sem=recv_sem,
        device_id={"coil": lax.rem(coil + 1, COILS)},
        device_id_type=MESH,
    )
    everything.wait_recv()
    total = outbox[coil]
    for slot in range(COILS - 1):
        total = total + inbox[slot]
    total = total * (COILS ** -0.5)
    gradient_ref[:half] = total
    gradient_ref[half:] = total[:2]
    everything.wait_send()


def finish(total_ref, misfit_ref, gradient_ref, residual_ref):
    half = OWN_ROWS // 2
    total = total_ref[:half]
    gradient_ref[:half, 0] = total[:, :OWN_COLS]
    gradient_ref[half:, 0] = pltpu.roll(total, 64, 1)[:, :OWN_COLS]
    residual_ref[0, 0] = misfit_ref[...]


def shards(*arguments):
    vmem = pl.BlockSpec(memory_space=pltpu.VMEM)
    anywhere = pl.BlockSpec(memory_space=pl.ANY)
    square = pltpu.VMEM((NPIX, NPIX), F32)
    own = pltpu.VMEM((NPIX, 128), F32)
    total, misfit = (
        pl.pallas_call(
            kernel,
            out_shape=(
                jax.ShapeDtypeStruct((8, 128), F32),
                jax.ShapeDtypeStruct((SROWS // NSEG, 2 * SCOLS), F32),
            ),
            in_specs=[anywhere] * 9,
            out_specs=(vmem, vmem),
            scratch_shapes=[
                pltpu.VMEM((NPIX, 2 * NPIX), BF16),
                pltpu.VMEM((NPIX, 2 * NPIX), BF16),
                square,
                pltpu.VMEM((SROWS, NPIX), BF16),
                pltpu.VMEM((SCOLS, NPIX), BF16),
                pltpu.VMEM((SROWS, 2 * SCOLS), BF16),
                pltpu.VMEM((2 * NPIX, NPIX), BF16),
                pltpu.VMEM((1, SROWS), jnp.int32),
                pltpu.SMEM((1,), jnp.int32),
                pltpu.VMEM((NPIX, NPIX), BF16),
                pltpu.VMEM((NPIX, NPIX), BF16),
                pltpu.VMEM((HALF, NPIX, NPIX), BF16),
                pltpu.VMEM((HALF, NPIX, NPIX), BF16),
                pltpu.VMEM((2 * NPIX + 16, 2 * SCOLS), BF16),
                pltpu.VMEM((4 * SROWS, NPIX), BF16),
                pltpu.VMEM((NPIX, 2 * SROWS), BF16),
                pltpu.VMEM((4 * BAND, 2 * SCOLS), BF16),
                pltpu.VMEM((4 * BAND, 2 * SCOLS), BF16),
                pltpu.VMEM((2 * SROWS, 2 * SCOLS), F32),
                pltpu.VMEM((HALF, SROWS, SCOLS), F32),
                pltpu.VMEM((HALF, SROWS, SCOLS), F32),
                pltpu.VMEM((SROWS, 2 * SCOLS), F32),
                own,
                own,
                own,
                own,
                own,
                own,
                pltpu.VMEM((2, SROWS, 128), F32),
                own,
                pltpu.VMEM((COILS, OWN_ROWS // 2, 128), F32),
                pltpu.VMEM((COILS - 1, OWN_ROWS // 2, 128), F32),
                pltpu.SemaphoreType.DMA((LOADS,)),
                pltpu.SemaphoreType.DMA,
                pltpu.SemaphoreType.DMA,
            ],
            compiler_params=pltpu.CompilerParams(
                collective_id=0, has_side_effects=True, vmem_limit_bytes=55160 * 2**10
            ),
        )(*arguments, jnp.asarray(dft_table()).astype(BF16))
    )

    gradient, residual = pl.pallas_call(
        finish,
        out_shape=(
            jax.ShapeDtypeStruct((OWN_ROWS, 1, OWN_COLS), F32),
            jax.ShapeDtypeStruct((1, 1, SROWS // NSEG, 2 * SCOLS), F32),
        ),
        in_specs=[vmem, vmem],
        out_specs=(vmem, vmem),
        compiler_params=pltpu.CompilerParams(vmem_limit_bytes=1 * 2**20),
    )(total, misfit)
    return jnp.transpose(gradient, (1, 0, 2)), residual


def solution(mesh):
    in_specs = (P(), P("coil", None, None), P(), P(), P(), P("coil", None, None, None), P(), P())
    out_specs = (P(None, "coil", "seg"), P("coil", None, "seg", None))
    return jax.shard_map(shards, mesh=mesh, in_specs=in_specs, out_specs=out_specs, check_vma=False)
```
